32 devices in a mesh: fsdp: 8 (over z, x), tok: 4 (over y, core).
Axes of the slice: x: 2, y: 2, z: 4, core: 2. Of those that a mesh axis runs over, the one named last changes fastest.
Arguments:
- tokens: bfloat16 [2, 8, 1024, 1024], P(None, 'fsdp', 'tok'), may hold values from -6 to 6
- cotangent: bfloat16 [2, 8, 1024, 1024], P(None, 'fsdp', 'tok'), may hold values from -6 to 6
- doc_lengths: int32 [2, 8, 4], P(None, 'fsdp'), may hold values from 0 to 1024, as said below
- norm1_gain: bfloat16 [1024], P('fsdp'), may hold values from 0.099609375 to 1.8984375
- norm1_shift: bfloat16 [1024], P('fsdp'), may hold values from -1.75 to 1.75
- w_qkv: bfloat16 [1024, 3072], P('fsdp'), may hold values from -0.1875 to 0.1875
- bias_query: bfloat16 [1024], P('fsdp'), may hold values from -1.75 to 1.75
- bias_value: bfloat16 [1024], P('fsdp'), may hold values from -1.75 to 1.75
- w_out: bfloat16 [1024, 1024], P('fsdp'), may hold values from -3 to 3
- bias_out: bfloat16 [1024], P('fsdp'), may hold values from -1.75 to 1.75
- norm2_gain: bfloat16 [1024], P('fsdp'), may hold values from 0.099609375 to 1.8984375
- norm2_shift: bfloat16 [1024], P('fsdp'), may hold values from -1.75 to 1.75
- w_fc1: bfloat16 [1024, 4096], P('fsdp'), may hold values from -0.1875 to 0.1875
- bias_fc1: bfloat16 [4096], P('fsdp'), may hold values from -1.75 to 1.75
- w_fc2: bfloat16 [4096, 1024], P('fsdp'), may hold values from -0.09375 to 0.09375
- bias_fc2: bfloat16 [1024], P('fsdp'), may hold values from -1.75 to 1.75
Outputs:
- output: bfloat16 [2, 8, 1024, 1024], P(None, 'fsdp', 'tok')
- grad_tokens: bfloat16 [2, 8, 1024, 1024], P(None, 'fsdp', 'tok')
- grad_norm1_gain: float32 [1024], P(('fsdp', 'tok'))
- grad_norm1_shift: float32 [1024], P(('fsdp', 'tok'))
- grad_w_qkv: float32 [1024, 3072], P(('fsdp', 'tok'))
- grad_bias_query: float32 [1024], P(('fsdp', 'tok'))
- grad_bias_value: float32 [1024], P(('fsdp', 'tok'))
- grad_w_out: float32 [1024, 1024], P(('fsdp', 'tok'))
- grad_bias_out: float32 [1024], P(('fsdp', 'tok'))
- grad_norm2_gain: float32 [1024], P(('fsdp', 'tok'))
- grad_norm2_shift: float32 [1024], P(('fsdp', 'tok'))
- grad_w_fc1: float32 [1024, 4096], P(('fsdp', 'tok'))
- grad_bias_fc1: float32 [4096], P(('fsdp', 'tok'))
- grad_w_fc2: float32 [4096, 1024], P(('fsdp', 'tok'))
- grad_bias_fc2: float32 [1024], P(('fsdp', 'tok'))
The draws below stay inside these ranges and needn't reach their ends.
Inputs may be any that keep to these rules, and one draw needn't show every extreme that they name: `doc_lengths`: each sequence's 4 lengths sum to 1024; a length 0 is an empty document. Among the 2 sequences of each index of fsdp, one is a single document.
All inputs are finite; a program needn't handle non-finite values.
Results may differ from the reference program's by a relative error of at most 0.013.
Values may be sent and summed in bfloat16 or wider, within the bound.
No kernel may reach another device: no remote copies, remote signals or barrier semaphores. Data moves between devices by JAX's collectives and lax.ppermute only.
A program may use at most 256 MiB of HBM per device.

```python
import jax
import jax.numpy as jnp
from jax import lax

D = 1024
H = 16
DH = 64
FF = 4096
SEQ = 1024
SPM = 1
MB = 2
NDOC = 4
NSEQ = 8


def draw_doc_lengths(key, part):
    key = jax.random.fold_in(key, 7)
    pick_key, share_key = jax.random.split(key)
    floor_len = SEQ // 16
    spare = SEQ - NDOC * floor_len
    raw = jax.random.randint(share_key, (MB, NSEQ, NDOC), 1, 1000)
    shares = raw * spare // jnp.sum(raw, axis=-1, keepdims=True)
    lengths = floor_len + shares
    last = SEQ - jnp.sum(lengths[..., :-1], axis=-1)
    lengths = jnp.concatenate([lengths[..., :-1], last[..., None]], axis=-1)
    chosen = jax.random.randint(pick_key, (NSEQ // SPM,), 0, MB * SPM)
    batch_pos = jnp.arange(MB, dtype=jnp.int32)[:, None]
    seq_pos = jnp.arange(NSEQ, dtype=jnp.int32)[None, :]
    code = batch_pos * SPM + seq_pos % SPM
    whole = code == chosen[seq_pos // SPM]
    single = jnp.where(jnp.arange(NDOC, dtype=jnp.int32) == 0, SEQ, 0)
    return jnp.where(whole[..., None], single[None, None, :], lengths).astype(jnp.int32)


def shard_levels(rng, dims, cuts, low, top_value):
    def one(position, parts):
        heights = jax.random.uniform(jax.random.fold_in(jax.random.fold_in(rng, 6), position), (parts,), jnp.float32, low / len(cuts), top_value / len(cuts))
        return jnp.repeat(jnp.exp(heights), dims[position] // parts).reshape((-1,) + (1,) * (len(dims) - position - 1))

    level = one(*cuts[0])
    for cut in cuts[1:]:
        level = level * one(*cut)
    return level


def normal_values(key, shape, width, most, cuts=(), kind=jnp.bfloat16):
    values = width * jax.random.normal(key, shape, jnp.float32)
    if cuts:
        values = values * shard_levels(key, shape, cuts, -0.22, 0.18)
    return jnp.clip(values, -most, most).astype(kind)


def setup_inputs(seed: int = 0) -> dict:
    key_list = jax.random.split(jax.random.key(seed), 17)
    return {
        "tokens": normal_values(key_list[0], (MB, NSEQ, SEQ, D), 1.0, 6.0, ((1, 8), (2, 4))),
        "cotangent": normal_values(key_list[1], (MB, NSEQ, SEQ, D), 1.0, 6.0, ((1, 8), (2, 4))),
        "doc_lengths": draw_doc_lengths(jax.random.fold_in(key_list[16], 71), 0),
        "norm1_gain": jnp.clip(1.0 + 0.18 * jax.random.normal(key_list[3], (D,), jnp.float32), 0.099609375, 1.8984375).astype(jnp.bfloat16),
        "norm1_shift": normal_values(key_list[4], (D,), 0.3, 1.75, ((0, 8),)),
        "w_qkv": normal_values(key_list[5], (D, 3 * D), D ** -0.5, 0.1875, ((0, 8),)),
        "bias_query": normal_values(key_list[6], (D,), 0.3, 1.75, ((0, 8),)),
        "bias_value": normal_values(key_list[7], (D,), 0.3, 1.75, ((0, 8),)),
        "w_out": normal_values(key_list[8], (D, D), (max(D // 256, 4)) ** -0.5, 3.0, ((0, 8),)),
        "bias_out": normal_values(key_list[9], (D,), 0.3, 1.75, ((0, 8),)),
        "norm2_gain": jnp.clip(1.0 + 0.18 * jax.random.normal(key_list[10], (D,), jnp.float32), 0.099609375, 1.8984375).astype(jnp.bfloat16),
        "norm2_shift": normal_values(key_list[11], (D,), 0.3, 1.75, ((0, 8),)),
        "w_fc1": normal_values(key_list[12], (D, FF), D ** -0.5, 0.1875, ((0, 8),)),
        "bias_fc1": normal_values(key_list[13], (FF,), 0.3, 1.75, ((0, 8),)),
        "w_fc2": normal_values(key_list[14], (FF, D), FF ** -0.5, 0.09375, ((0, 8),)),
        "bias_fc2": normal_values(key_list[15], (D,), 0.3, 1.75, ((0, 8),)),
    }


@jax.custom_vjp
def low(v):
    return lax.optimization_barrier(v.astype(jnp.bfloat16)).astype(jnp.float32)

@jax.custom_vjp
def low_back(v):
    return v

def low_keep(v):
    return (low(v), None)

def low_pass(kept, grad):
    return (grad,)

def back_keep(v):
    return (v, None)

def back_low(kept, grad):
    return (low(grad),)
low.defvjp(low_keep, low_pass)
low_back.defvjp(back_keep, back_low)
eps = 1e-05
masked_value = -1e+30
highest = lax.Precision.HIGHEST

def layer_norm(values, gain, shift):
    mean = lax.optimization_barrier(jnp.mean(values, axis=-1, keepdims=True))
    centered = values - mean
    spread = lax.optimization_barrier(jnp.mean(centered * centered, axis=-1, keepdims=True))
    return centered * lax.rsqrt(spread + eps) * gain + shift

def doc_allowed(lengths):
    ends = jnp.cumsum(lengths, axis=-1)
    positions = jnp.arange(SEQ, dtype=jnp.int32)
    docs = lax.optimization_barrier(jnp.sum((positions[:, None] >= ends[None, :]).astype(jnp.int32), axis=-1))
    causal = positions[None, :] <= positions[:, None]
    return causal & (docs[:, None] == docs[None, :])

def block(inputs, params, allowed):
    norm1_gain, norm1_shift, w_qkv, bias_query, bias_value, w_out, bias_out, norm2_gain, norm2_shift, w_fc1, bias_fc1, w_fc2, bias_fc2 = params
    normed = low(layer_norm(inputs, norm1_gain, norm1_shift))
    mixed = jnp.dot(normed, w_qkv, precision=highest)
    query = low(low_back(mixed[:, :D] + bias_query))
    key = low(low_back(mixed[:, D:2 * D]))
    value = low(low_back(mixed[:, 2 * D:] + bias_value))
    query_h = query.reshape(SEQ, H, DH)
    key_h = key.reshape(SEQ, H, DH)
    value_h = value.reshape(SEQ, H, DH)
    scores = jnp.einsum('qhd,khd->hqk', query_h, key_h, precision=highest) * DH ** (-0.5)
    scores = low_back(scores)
    scores = jnp.where(allowed[None], scores, masked_value)
    shifted = scores - lax.optimization_barrier(jnp.max(scores, axis=-1, keepdims=True))
    expo = jnp.exp(shifted)
    probs = low(expo / lax.optimization_barrier(jnp.sum(expo, axis=-1, keepdims=True)))
    attended = jnp.einsum('hqk,khd->qhd', probs, value_h, precision=highest).reshape(SEQ, D)
    attended = low(low_back(attended))
    branch = low_back(jnp.dot(attended, w_out, precision=highest) + bias_out)
    middle = inputs + branch
    normed2 = low(layer_norm(middle, norm2_gain, norm2_shift))
    hidden = low_back(jnp.dot(normed2, w_fc1, precision=highest) + bias_fc1)
    active = low(jax.nn.gelu(hidden, approximate=True))
    second = low_back(jnp.dot(active, w_fc2, precision=highest) + bias_fc2)
    return middle + second

def reference(tokens, cotangent, doc_lengths, norm1_gain, norm1_shift, w_qkv, bias_query, bias_value, w_out, bias_out, norm2_gain, norm2_shift, w_fc1, bias_fc1, w_fc2, bias_fc2):
    params = (norm1_gain, norm1_shift, w_qkv, bias_query, bias_value, w_out, bias_out, norm2_gain, norm2_shift, w_fc1, bias_fc1, w_fc2, bias_fc2)
    params = tuple((p.astype(jnp.float32) for p in params))
    inputs_all = tokens.astype(jnp.float32).reshape(MB * NSEQ, SEQ, D)
    upstream_all = cotangent.astype(jnp.float32).reshape(MB * NSEQ, SEQ, D)
    lengths_all = doc_lengths.reshape(MB * NSEQ, NDOC)

    def one_sequence(totals, item):
        inputs, upstream, lengths = item
        allowed = doc_allowed(lengths)
        result, pull = jax.vjp(lambda v, p: block(v, p, allowed), inputs, params)
        grad_in, grad_params = pull(upstream)
        totals = tuple((a + b for a, b in zip(totals, grad_params)))
        return (totals, (result.astype(jnp.bfloat16), grad_in.astype(jnp.bfloat16)))
    zeros = tuple((jnp.zeros_like(p) for p in params))
    grads, (results, grad_ins) = lax.scan(one_sequence, zeros, (inputs_all, upstream_all, lengths_all))
    return (results.reshape(tokens.shape), grad_ins.reshape(tokens.shape), grads[0], grads[1], grads[2], grads[3], grads[4], grads[5], grads[6], grads[7], grads[8], grads[9], grads[10], grads[11], grads[12])
```

```python
import functools

import jax
import jax.numpy as jnp
from jax import lax
from jax.experimental import pallas as pl
from jax.experimental.pallas import tpu as pltpu
from jax.sharding import PartitionSpec as P

DH = 64
PAIR = 2 * DH
eps = 1e-05
masked_value = -1e30
f32 = jnp.float32
bf16 = jnp.bfloat16
AXES = ("fsdp", "tok")


class Grid:
    def __init__(self, n_fsdp, n_tok):
        self.n_fsdp, self.n_tok = n_fsdp, n_tok
        self.nz, self.ny = n_fsdp // 2, n_tok // 2
        self.f, self.t = lax.axis_index("fsdp"), lax.axis_index("tok")
        self.z, self.x = self.f // 2, self.f % 2
        self.y, self.c = self.t // 2, self.t % 2

    def send(self, value, place):
        pairs = []
        for f in range(self.n_fsdp):
            for t in range(self.n_tok):
                z, x, y, c = place(f // 2, f % 2, t // 2, t % 2)
                pairs.append((f * self.n_tok + t, (z * 2 + x) * self.n_tok + y * 2 + c))
        return lax.ppermute(value, AXES, pairs)

    def over_core(self, value):
        return self.send(value, lambda z, x, y, c: (z, x, y, 1 - c))

    def over_x(self, value):
        return self.send(value, lambda z, x, y, c: (z, 1 - x, y, c))

    def over_y(self, value):
        return self.send(value, lambda z, x, y, c: (z, x, 1 - y, c))

    def over_yc(self, value):
        return self.send(value, lambda z, x, y, c: (z, x, 1 - y, 1 - c))

    def over_z(self, value, shift):
        return self.send(value, lambda z, x, y, c: ((z + shift) % self.nz, x, y, c))


def pick(values, index, axis):
    return lax.dynamic_index_in_dim(values, index, axis, keepdims=False)


def both(a, b):
    return (a.astype(f32) + b.astype(f32)).astype(bf16)


def place_kernel(rows, offsets, *refs):
    pieces, out, sem = refs[:-2], refs[-2], refs[-1]
    copies = []
    at = 0
    for piece in pieces:
        for j in range(piece.shape[0]):
            first = pl.multiple_of(offsets[at], rows)
            copies.append(pltpu.make_async_copy(piece.at[j], out.at[pl.ds(first, rows)], sem.at[at]))
            at += 1
    for copy in copies:
        copy.start()
    for copy in copies:
        copy.wait()


def gather_weight(grid, shard):
    shard_rows, width = shard.shape
    rows = shard_rows // grid.n_tok
    if grid.nz != 4 or grid.ny != 2 or rows % 16:
        return lax.all_gather(shard, "fsdp", axis=0, tiled=True)
    own = lax.dynamic_slice_in_dim(shard, grid.t * rows, rows, 0)
    steps = [own] + [grid.over_z(own, k) for k in (1, 2, 3)]
    qa, qb = jnp.stack(steps[:2]), jnp.stack(steps[2:])
    xa, yb = grid.over_x(qa), grid.over_y(qb)
    ya, xb = grid.over_y(qa), grid.over_x(qb)
    xya, xyb = grid.over_y(xa), grid.over_x(yb)
    have = [
        (qa, 0, 0, 0), (qb, 2, 0, 0), (xa, 0, 1, 0), (yb, 2, 0, 1),
        (ya, 0, 0, 1), (xb, 2, 1, 0), (xya, 0, 1, 1), (xyb, 2, 1, 1),
    ]
    pieces, offsets = [], []
    for piece, k, dx, dy in have:
        for dc in (0, 1):
            pieces.append(grid.over_core(piece) if dc else piece)
            for j in range(2):
                z = (grid.z + 4 - k - j) % 4
                x, y, c = grid.x ^ dx, grid.y ^ dy, grid.c ^ dc
                offsets.append((z * 2 + x) * shard_rows + (y * 2 + c) * rows)
    total = grid.n_fsdp * shard_rows
    return pl.pallas_call(
        functools.partial(place_kernel, rows),
        out_shape=jax.ShapeDtypeStruct((total, width), shard.dtype),
        in_specs=[pl.BlockSpec(memory_space=pltpu.SMEM)]
        + [pl.BlockSpec(memory_space=pl.ANY)] * len(pieces),
        out_specs=pl.BlockSpec(memory_space=pltpu.VMEM),
        scratch_shapes=[pltpu.SemaphoreType.DMA((len(offsets),))],
        compiler_params=pltpu.CompilerParams(vmem_limit_bytes=20 * 2**20),
        cost_estimate=pl.CostEstimate(
            flops=0, bytes_accessed=4 * total * width, transcendentals=0
        ),
        name="place",
    )(jnp.stack(offsets).astype(jnp.int32), *pieces)


def gather_vectors(grid, packed):
    if grid.nz != 4:
        return lax.all_gather(packed, "fsdp", axis=0)
    whole = jnp.zeros((grid.n_fsdp,) + packed.shape, packed.dtype)
    whole = lax.dynamic_update_index_in_dim(whole, packed, grid.f, 0)
    whole = whole + grid.over_x(whole)
    whole = whole + grid.over_z(whole, 1)
    return whole + grid.over_z(whole, 2)


def scatter_grad(grid, grad):
    rows = grad.shape[0] // (grid.n_fsdp * grid.n_tok)
    if grid.nz != 4 or grid.ny != 2 or rows % 16:
        return lax.psum_scatter(grad.astype(f32), AXES, scatter_dimension=0, tiled=True)
    grad = grad.astype(bf16)
    width = grad.shape[1]
    parts = grad.reshape(4, 2, 2, 2, rows, width)
    z, x, y, c = grid.z, grid.x, grid.y, grid.c
    pa, pb = parts[:2], parts[2:]
    ha = both(pick(pa, c, 3), grid.over_core(pick(pa, 1 - c, 3)))
    hb = both(pick(pb, c, 3), grid.over_core(pick(pb, 1 - c, 3)))
    a1 = both(pick(ha, x, 1), grid.over_x(pick(ha, 1 - x, 1)))
    b1 = both(pick(hb, y, 2), grid.over_y(pick(hb, 1 - y, 2)))
    a2 = both(pick(a1, y, 1), grid.over_y(pick(a1, 1 - y, 1)))
    b2 = both(pick(b1, x, 1), grid.over_x(pick(b1, 1 - x, 1)))
    last = jnp.concatenate([a2, b2], axis=0)
    total = pick(last, z, 0).astype(f32)
    for shift in (1, 2, 3):
        total = total + grid.over_z(pick(last, (z + shift) % 4, 0), shift).astype(f32)
    return total


def sum_vectors(grid, packed):
    if grid.nz != 4 or grid.ny != 2:
        return lax.psum(packed, AXES)
    packed = packed + grid.over_core(packed)
    packed = packed + grid.over_x(packed)
    packed = packed + grid.over_y(packed)
    return packed + grid.over_z(packed, 1) + grid.over_z(packed, 2) + grid.over_z(packed, 3)


def layer_norm(values, gain, shift):
    mean = jnp.mean(values, axis=-1, keepdims=True)
    centered = values - mean
    spread = jnp.mean(centered * centered, axis=-1, keepdims=True)
    return centered * lax.rsqrt(spread + eps) * gain + shift


def norm_back(values, gain, shift, upstream):
    result, pull = jax.vjp(layer_norm, values, gain, shift)
    return pull(upstream)


def smooth_gate(values):
    return jax.nn.gelu(values, approximate=True)


def by_rows(a, b):
    return lax.dot_general(a, b, (((1,), (1,)), ((), ())), preferred_element_type=f32)


def by_columns(a, b):
    return lax.dot_general(a, b, (((0,), (0,)), ((), ())), preferred_element_type=f32)


def fill(info, own, other, whole, block):
    for j in range(2):
        rows = slice(j * block, (j + 1) * block)
        whole[pl.ds(pl.multiple_of(info[j] * block, block), block), :] = own[rows, :]
        whole[pl.ds(pl.multiple_of(info[2 + j] * block, block), block), :] = other[rows, :]


def head_part(values, h):
    lane = lax.broadcasted_iota(jnp.int32, values.shape, 1)
    return jnp.where(lane // DH == h, values, jnp.zeros_like(values))


def keep_mask(starts, index, first, keys, block):
    key_pos = lax.broadcasted_iota(jnp.int32, (keys, block), 0)
    query_pos = first + lax.broadcasted_iota(jnp.int32, (1, block), 1)
    start = starts[pl.ds(index, 1), :]
    return (key_pos >= start) & (key_pos <= query_pos)


def attend_kernel(block, info, starts, q, k, v, ko, vo, out, lse, kn, vn):
    fill(info, k, ko, kn, block)
    fill(info, v, vo, vn, block)

    def run(index, count):
        at = pl.ds(pl.multiple_of(index * block, block), block)
        keys, vals = kn[: count * block, :], vn[: count * block, :]
        query = q[at, :] * jnp.asarray(DH**-0.5, bf16)
        keep = keep_mask(starts, index, info[index] * block, count * block, block)
        sides = []
        for h in range(2):
            scores = jnp.where(keep, by_rows(keys, head_part(query, h)), masked_value)
            top = jnp.max(scores, axis=0, keepdims=True)
            expo = jnp.exp(scores - top)
            total = jnp.sum(expo, axis=0, keepdims=True)
            lse[0, pl.ds(2 * h + index, 1), :] = top + jnp.log(total)
            side = by_columns(vals, expo.astype(bf16)) / total
            sides.append(side[h * DH : (h + 1) * DH])
        out[at, :] = jnp.concatenate(sides, axis=0).T.astype(bf16)

    low = info[4]
    for index, counts in ((low, (1, 2)), (1 - low, (3, 4))):
        for count in counts:
            pl.when(info[index] == count - 1)(functools.partial(run, index, count))


def attend_back_kernel(
    block, info, starts, q, k, v, ko, vo, out, lse, grad, dq, dk, dv, dko, dvo, kn, vn, dkn, dvn
):
    fill(info, k, ko, kn, block)
    fill(info, v, vo, vn, block)
    dkn[...] = jnp.zeros_like(dkn)
    dvn[...] = jnp.zeros_like(dvn)

    def run(index, count):
        at = pl.ds(pl.multiple_of(index * block, block), block)
        keys, vals = kn[: count * block, :], vn[: count * block, :]
        query = q[at, :] * jnp.asarray(DH**-0.5, bf16)
        up = grad[at, :]
        product = (up.astype(f32) * out[at, :].astype(f32)).T
        keep = keep_mask(starts, index, info[index] * block, count * block, block)
        sides = []
        for h in range(2):
            query_h, up_h = head_part(query, h), head_part(up, h)
            inner = jnp.sum(product[h * DH : (h + 1) * DH], axis=0, keepdims=True)
            scores = jnp.where(keep, by_rows(keys, query_h), masked_value)
            probs = jnp.exp(scores - lse[0, pl.ds(2 * h + index, 1), :])
            grad_scores = (probs * (by_rows(vals, up_h) - inner)).astype(bf16)
            dvn[: count * block, :] += jnp.dot(
                probs.astype(bf16), up_h, preferred_element_type=f32
            )
            dkn[: count * block, :] += jnp.dot(grad_scores, query_h, preferred_element_type=f32)
            side = by_columns(keys, grad_scores) * DH**-0.5
            sides.append(side[h * DH : (h + 1) * DH])
        dq[at, :] = jnp.concatenate(sides, axis=0).T.astype(bf16)

    low = info[4]
    for index, counts in ((low, (1, 2)), (1 - low, (3, 4))):
        for count in counts:
            pl.when(info[index] == count - 1)(functools.partial(run, index, count))
    for j in range(2):
        rows = slice(j * block, (j + 1) * block)
        own = pl.ds(pl.multiple_of(info[j] * block, block), block)
        other = pl.ds(pl.multiple_of(info[2 + j] * block, block), block)
        dk[rows, :], dv[rows, :] = dkn[own, :], dvn[own, :]
        dko[rows, :], dvo[rows, :] = dkn[other, :].astype(bf16), dvn[other, :].astype(bf16)


def attend_specs(count, width):
    pairs = width // PAIR
    return [
        pl.BlockSpec(starts_shape, lambda h, info: (0, 0)) for starts_shape in ((2, count // 2),)
    ] + [
        pl.BlockSpec((count, PAIR), lambda h, info: (0, h)),
        pl.BlockSpec((count, PAIR), lambda h, info: (0, pairs + h)),
        pl.BlockSpec((count, PAIR), lambda h, info: (0, 2 * pairs + h)),
        pl.BlockSpec((count, PAIR), lambda h, info: (0, h)),
        pl.BlockSpec((count, PAIR), lambda h, info: (0, pairs + h)),
    ]


def attend(info, starts, mixed, other):
    count, width = mixed.shape[0], mixed.shape[1] // 3
    pairs, block = width // PAIR, count // 2
    column = pl.BlockSpec((count, PAIR), lambda h, info: (0, h))
    return pl.pallas_call(
        functools.partial(attend_kernel, block),
        out_shape=(
            jax.ShapeDtypeStruct((count, width), bf16),
            jax.ShapeDtypeStruct((pairs, 4, block), f32),
        ),
        grid_spec=pltpu.PrefetchScalarGridSpec(
            num_scalar_prefetch=1,
            grid=(pairs,),
            in_specs=attend_specs(count, width),
            out_specs=[column, pl.BlockSpec((1, 4, block), lambda h, info: (h, 0, 0))],
            scratch_shapes=[pltpu.VMEM((2 * count, PAIR), bf16)] * 2,
        ),
        compiler_params=pltpu.CompilerParams(vmem_limit_bytes=32 * 2**20),
        cost_estimate=pl.CostEstimate(
            flops=8 * count * count * width, bytes_accessed=12 * count * width,
            transcendentals=20 * count * count,
        ),
        name="attend",
    )(info, starts, mixed, mixed, mixed, other, other)


def attend_back(info, starts, mixed, other, attended, lse, grad):
    count, width = attended.shape
    pairs, block = width // PAIR, count // 2
    column = pl.BlockSpec((count, PAIR), lambda h, info: (0, h))
    return pl.pallas_call(
        functools.partial(attend_back_kernel, block),
        out_shape=tuple(
            jax.ShapeDtypeStruct((count, width), kind) for kind in (bf16, f32, f32, bf16, bf16)
        ),
        grid_spec=pltpu.PrefetchScalarGridSpec(
            num_scalar_prefetch=1,
            grid=(pairs,),
            in_specs=attend_specs(count, width)
            + [column, pl.BlockSpec((1, 4, block), lambda h, info: (h, 0, 0)), column],
            out_specs=[column] * 5,
            scratch_shapes=[pltpu.VMEM((2 * count, PAIR), bf16)] * 2
            + [pltpu.VMEM((2 * count, PAIR), f32)] * 2,
        ),
        compiler_params=pltpu.CompilerParams(vmem_limit_bytes=32 * 2**20),
        cost_estimate=pl.CostEstimate(
            flops=20 * count * count * width, bytes_accessed=28 * count * width,
            transcendentals=20 * count * count,
        ),
        name="attend_back",
    )(info, starts, mixed, mixed, mixed, other, other, attended, lse, grad)


def local(
    n_fsdp,
    n_tok,
    tokens,
    cotangent,
    doc_lengths,
    norm1_gain,
    norm1_shift,
    w_qkv,
    bias_query,
    bias_value,
    w_out,
    bias_out,
    norm2_gain,
    norm2_shift,
    w_fc1,
    bias_fc1,
    w_fc2,
    bias_fc2,
):
    grid = Grid(n_fsdp, n_tok)
    y, t = grid.y, grid.t
    block, width = tokens.shape[2:]
    hidden_width = w_fc1.shape[1]

    def swap(values):
        mine, theirs = pick(values, y, 0)[0], pick(values, 1 - y, 0)[0]
        return jnp.concatenate([mine, grid.over_yc(theirs)], axis=0)

    def swap_back(values):
        mine, back = values[:block], grid.over_yc(values[block:])
        first, second = jnp.where(y == 0, mine, back), jnp.where(y == 0, back, mine)
        return jnp.stack([first, second])[:, None]

    rows = swap(tokens)
    full_qkv = gather_weight(grid, w_qkv)
    vectors = (
        norm1_gain, norm1_shift, bias_query, bias_value, bias_out, norm2_gain, norm2_shift, bias_fc2
    )
    part = norm1_gain.shape[0]
    packed = jnp.concatenate([v[None] for v in vectors] + [bias_fc1.reshape(-1, part)], axis=0)
    packed = gather_vectors(grid, packed)
    gain1, shift1, b_query, b_value, b_out, gain2, shift2, b_fc2 = (
        packed[:, i].reshape(width).astype(f32) for i in range(8)
    )
    b_fc1 = packed[:, 8:].reshape(hidden_width).astype(f32)
    upstream = swap(cotangent)
    full_out = gather_weight(grid, w_out)
    full_fc1 = gather_weight(grid, w_fc1)
    full_fc2 = gather_weight(grid, w_fc2)

    mine, across = jnp.stack([t, 3 - t]), jnp.stack([t ^ 1, 3 - (t ^ 1)])
    info = jnp.concatenate([mine, across, y[None]]).astype(jnp.int32)
    lengths = pick(doc_lengths, y, 0)[0]
    ends = jnp.cumsum(lengths)
    place = mine[:, None] * block + jnp.arange(block, dtype=jnp.int32)[None]
    starts = jnp.max(
        jnp.where(place[..., None] >= ends, ends, 0), axis=-1
    ).astype(jnp.int32)

    inputs = rows.astype(f32)
    normed = layer_norm(inputs, gain1, shift1).astype(bf16)
    b_qkv = jnp.concatenate([b_query, jnp.zeros_like(b_query), b_value])
    mixed = (jnp.dot(normed, full_qkv, preferred_element_type=f32) + b_qkv).astype(bf16)
    other = grid.over_core(mixed[:, width:])
    attended, lse = attend(info, starts, mixed, other)
    middle = inputs + jnp.dot(attended, full_out, preferred_element_type=f32) + b_out
    normed2 = layer_norm(middle, gain2, shift2).astype(bf16)
    hidden = jnp.dot(normed2, full_fc1, preferred_element_type=f32) + b_fc1
    active = smooth_gate(hidden).astype(bf16)
    result = middle + jnp.dot(active, full_fc2, preferred_element_type=f32) + b_fc2
    output = swap_back(result.astype(bf16))

    def weight_grad(left, right):
        return lax.dot_general(
            left, right, (((0,), (0,)), ((), ())), preferred_element_type=f32
        ).astype(bf16)

    def back(left, weight):
        return lax.dot_general(
            left, weight, (((1,), (1,)), ((), ())), preferred_element_type=f32
        )

    grad_out = upstream.astype(f32)
    grad_fc2 = scatter_grad(grid, weight_grad(active, upstream))
    grad_bias_fc2 = jnp.sum(grad_out, axis=0)
    unused, gate_pull = jax.vjp(smooth_gate, hidden)
    grad_hidden = gate_pull(back(upstream, full_fc2))[0].astype(bf16)
    grad_fc1 = scatter_grad(grid, weight_grad(normed2, grad_hidden))
    grad_bias_fc1 = jnp.sum(grad_hidden.astype(f32), axis=0)
    grad_mid_norm, grad_gain2, grad_shift2 = norm_back(
        middle, gain2, shift2, back(grad_hidden, full_fc1)
    )
    grad_middle = grad_out + grad_mid_norm
    grad_branch = grad_middle.astype(bf16)
    grad_w_out = scatter_grad(grid, weight_grad(attended, grad_branch))
    grad_bias_out = jnp.sum(grad_branch.astype(f32), axis=0)
    grad_attended = back(grad_branch, full_out).astype(bf16)
    dq, dk, dv, dko, dvo = attend_back(
        info, starts, mixed, other, attended, lse, grad_attended
    )
    dk = (dk + grid.over_core(dko).astype(f32)).astype(bf16)
    dv = (dv + grid.over_core(dvo).astype(f32)).astype(bf16)
    grad_mixed = jnp.concatenate([dq, dk, dv], axis=1)
    grad_qkv = scatter_grad(grid, weight_grad(normed, grad_mixed))
    grad_bias_query = jnp.sum(dq.astype(f32), axis=0)
    grad_bias_value = jnp.sum(dv.astype(f32), axis=0)
    grad_in_norm, grad_gain1, grad_shift1 = norm_back(
        inputs, gain1, shift1, back(grad_mixed, full_qkv)
    )
    grad_tokens = swap_back((grad_middle + grad_in_norm).astype(bf16))

    sums = jnp.concatenate(
        [
            v.reshape(-1, width)
            for v in (
                grad_gain1, grad_shift1, grad_bias_query, grad_bias_value, grad_bias_out,
                grad_gain2, grad_shift2, grad_bias_fc2, grad_bias_fc1,
            )
        ],
        axis=0,
    )
    sums = sum_vectors(grid, sums)
    device, devices = grid.f * n_tok + t, n_fsdp * n_tok

    def owned(vector):
        count = vector.shape[0] // devices
        return lax.dynamic_slice_in_dim(vector, device * count, count, 0)

    return (
        output,
        grad_tokens,
        owned(sums[0]),
        owned(sums[1]),
        grad_qkv,
        owned(sums[2]),
        owned(sums[3]),
        grad_w_out,
        owned(sums[4]),
        owned(sums[5]),
        owned(sums[6]),
        grad_fc1,
        owned(sums[8:].reshape(hidden_width)),
        grad_fc2,
        owned(sums[7]),
    )


def solution(mesh):
    vector, matrix = P("fsdp"), P("fsdp", None)
    rows = P(None, "fsdp", "tok", None)
    own_vector, own_matrix = P(("fsdp", "tok")), P(("fsdp", "tok"), None)
    return jax.shard_map(
        functools.partial(local, mesh.shape["fsdp"], mesh.shape["tok"]),
        mesh=mesh,
        in_specs=(
            rows, rows, P(None, "fsdp", None), vector, vector, matrix, vector, vector,
            matrix, vector, vector, vector, matrix, vector, matrix, vector,
        ),
        out_specs=(
            rows, rows, own_vector, own_vector, own_matrix, own_vector, own_vector,
            own_matrix, own_vector, own_vector, own_vector, own_matrix, own_vector,
            own_matrix, own_vector,
        ),
        check_vma=False,
    )
```

```python
import functools

import jax
import jax.numpy as jnp
from jax import lax
from jax.experimental import pallas as pl
from jax.experimental.pallas import tpu as pltpu
from jax.sharding import PartitionSpec as P

DH = 64
PAIR = 2 * DH
eps = 1e-05
masked_value = -1e30
f32 = jnp.float32
bf16 = jnp.bfloat16
AXES = ("fsdp", "tok")


class Grid:
    def __init__(self, n_fsdp, n_tok):
        self.n_fsdp, self.n_tok = n_fsdp, n_tok
        self.nz, self.ny = n_fsdp // 2, n_tok // 2
        self.f, self.t = lax.axis_index("fsdp"), lax.axis_index("tok")
        self.z, self.x = self.f // 2, self.f % 2
        self.y, self.c = self.t // 2, self.t % 2

    def staged(self, rows):
        return self.nz == 4 and self.ny == 2 and rows % 16 == 0

    def send(self, value, place):
        pairs = []
        for f in range(self.n_fsdp):
            for t in range(self.n_tok):
                z, x, y, c = place(f // 2, f % 2, t // 2, t % 2)
                pairs.append((f * self.n_tok + t, (z * 2 + x) * self.n_tok + y * 2 + c))
        return lax.ppermute(value, AXES, pairs)

    def over_core(self, value):
        return self.send(value, lambda z, x, y, c: (z, x, y, 1 - c))

    def over_x(self, value):
        return self.send(value, lambda z, x, y, c: (z, 1 - x, y, c))

    def over_y(self, value):
        return self.send(value, lambda z, x, y, c: (z, x, 1 - y, c))

    def over_yc(self, value):
        return self.send(value, lambda z, x, y, c: (z, x, 1 - y, 1 - c))

    def flip_z(self, value, bit):
        return self.send(value, lambda z, x, y, c: (z ^ bit, x, y, c))

    def over_z(self, value, shift):
        return self.send(value, lambda z, x, y, c: ((z + shift) % self.nz, x, y, c))


def pick(values, index, axis):
    return lax.dynamic_index_in_dim(values, index, axis, keepdims=False)


def both(a, b):
    return (a.astype(f32) + b.astype(f32)).astype(bf16)


def halves(a, b, index):
    keep, send = index, 1 - index
    return both(pick(a, keep, 0), pick(b, keep, 0)), both(pick(a, send, 0), pick(b, send, 0))


def place_kernel(rows, widths, offsets, *refs):
    sem, outs, pieces = refs[-1], refs[-1 - len(widths) : -1], refs[: -1 - len(widths)]
    copies = []
    at = 0
    for piece in pieces:
        for j in range(piece.shape[0]):
            first = pl.multiple_of(offsets[at], rows)
            column = 0
            for i, width in enumerate(widths):
                copies.append(
                    pltpu.make_async_copy(
                        piece.at[j, :, pl.ds(column, width)],
                        outs[i].at[pl.ds(first, rows)],
                        sem.at[at * len(widths) + i],
                    )
                )
                column += width
            at += 1
    for copy in copies:
        copy.start()
    for copy in copies:
        copy.wait()


class Gather:
    def __init__(self, grid, *shards):
        self.grid, self.shards = grid, shards
        self.rows = shards[0].shape[0] // grid.n_tok
        self.staged = grid.staged(self.rows)
        self.state = {"shards": list(shards)}
        self.flip = True

    def own(self):
        parts = [
            lax.dynamic_slice_in_dim(w, self.grid.t * self.rows, self.rows, 0)
            for w in self.state["shards"]
        ]
        return jnp.concatenate(parts, axis=1)

    def along_z(self):
        if self.staged:
            own = self.own()
            self.flip = False
            self.state = {"steps": [own] + [self.grid.over_z(own, k) for k in (1, 2, 3)]}

    def near_z(self):
        if self.staged:
            own = self.own()
            self.state = {"steps": [own, self.grid.flip_z(own, 1)]}

    def far_z(self):
        if self.staged:
            two = jnp.stack(self.state["steps"])
            self.state = {"steps": [two, self.grid.flip_z(two, 2)]}

    def first(self):
        if self.staged:
            grid, steps = self.grid, self.state["steps"]
            q = jnp.concatenate(steps) if self.flip else jnp.stack(steps)
            self.state = {
                "q": q, "x": grid.over_x(q), "y": grid.over_y(q), "cq": grid.over_core(q)
            }

    def second(self):
        if self.staged:
            state, grid = self.state, self.grid
            state["a"], state["b"] = grid.over_y(state["x"][:2]), grid.over_x(state["y"][2:])
            state["cxy"] = grid.over_core(jnp.concatenate([state["x"], state["y"]]))

    def last(self):
        if self.staged:
            state = self.state
            state["cab"] = self.grid.over_core(jnp.concatenate([state["a"], state["b"]]))

    def place(self):
        if not self.staged:
            return [lax.all_gather(w, "fsdp", axis=0, tiled=True) for w in self.state["shards"]]
        grid, rows = self.grid, self.rows
        shard_rows, kind = self.shards[0].shape[0], self.shards[0].dtype
        widths = [w.shape[1] for w in self.shards]
        at = lambda dx, dy: [(k, dx, dy) for k in range(4)]
        ab = at(1, 1)
        order = (
            ("q", at(0, 0), 0), ("x", at(1, 0), 0), ("y", at(0, 1), 0), ("a", ab[:2], 0),
            ("b", ab[2:], 0), ("cq", at(0, 0), 1), ("cxy", at(1, 0) + at(0, 1), 1), ("cab", ab, 1),
        )
        offsets = []
        for name, places, dc in order:
            for k, dx, dy in places:
                z = grid.z ^ k if self.flip else (grid.z + 4 - k) % 4
                x, y, c = grid.x ^ dx, grid.y ^ dy, grid.c ^ dc
                offsets.append((z * 2 + x) * shard_rows + (y * 2 + c) * rows)
        total = grid.n_fsdp * shard_rows
        return pl.pallas_call(
            functools.partial(place_kernel, rows, widths),
            out_shape=[jax.ShapeDtypeStruct((total, width), kind) for width in widths],
            in_specs=[pl.BlockSpec(memory_space=pltpu.SMEM)]
            + [pl.BlockSpec(memory_space=pl.ANY)] * len(order),
            out_specs=[pl.BlockSpec(memory_space=pltpu.VMEM)] * len(widths),
            scratch_shapes=[pltpu.SemaphoreType.DMA((len(offsets) * len(widths),))],
            compiler_params=pltpu.CompilerParams(vmem_limit_bytes=24 * 2**20),
            cost_estimate=pl.CostEstimate(
                flops=0, bytes_accessed=4 * total * sum(widths), transcendentals=0
            ),
            name="place",
        )(jnp.stack(offsets).astype(jnp.int32), *(self.state[name] for name, *_ in order))


class GatherVectors:
    def __init__(self, grid, packed):
        self.grid, self.staged = grid, grid.nz == 4
        self.state = packed

    def over_x(self):
        if not self.staged:
            self.state = lax.all_gather(self.state, "fsdp", axis=0)
            return
        whole = jnp.zeros((self.grid.n_fsdp,) + self.state.shape, self.state.dtype)
        whole = lax.dynamic_update_index_in_dim(whole, self.state, self.grid.f, 0)
        self.state = whole + self.grid.over_x(whole)

    def over_z(self, bit):
        if self.staged:
            self.state = self.state + self.grid.flip_z(self.state, bit)


def split_kernel(rows, core, left, right, own, other):
    total = by_columns(left[...], right[...]).astype(bf16)
    first = core[0] == 0

    def put(order):
        for x in range(2):
            for y in range(2):
                at = (x * 2 + y) * 2 * rows
                low, high = total[at : at + rows], total[at + rows : at + 2 * rows]
                i, j = (x, y) if order else (y, x)
                own[0, i, j, 0] = jnp.where(first, low, high)
                other[0, i, j, 0] = jnp.where(first, high, low)

    z = pl.program_id(1)
    pl.when(z < 2)(lambda: put(True))
    pl.when(z >= 2)(lambda: put(False))


class Scatter:
    def __init__(self, grid, left, right):
        self.grid = grid
        count, height, width = left.shape + right.shape[1:]
        rows = height // (grid.n_fsdp * grid.n_tok)
        self.staged = grid.staged(rows)
        if not self.staged:
            self.state = by_columns(left, right)
            return
        tile = min(width, 2**18 // (8 * rows))
        part = jax.ShapeDtypeStruct((2, 2, 2, 2, rows, width), bf16)
        block = pl.BlockSpec(
            (1, 2, 2, 1, rows, tile), lambda n, z, core: (z // 2, 0, 0, z % 2, 0, n)
        )
        self.state = pl.pallas_call(
            functools.partial(split_kernel, rows),
            out_shape=(part, part),
            grid_spec=pltpu.PrefetchScalarGridSpec(
                num_scalar_prefetch=1,
                grid=(width // tile, 4),
                in_specs=[
                    pl.BlockSpec((count, 8 * rows), lambda n, z, core: (0, z)),
                    pl.BlockSpec((count, tile), lambda n, z, core: (0, n)),
                ],
                out_specs=[block, block],
            ),
            compiler_params=pltpu.CompilerParams(vmem_limit_bytes=32 * 2**20),
            cost_estimate=pl.CostEstimate(
                flops=2 * count * height * width,
                bytes_accessed=2 * (height * width + count * (height + width)),
                transcendentals=0,
            ),
            name="grad_split",
        )(grid.c[None].astype(jnp.int32), left, right)

    def core(self):
        if self.staged:
            own, other = self.state
            self.state = (own, self.grid.over_core(other))

    def first(self):
        if self.staged:
            grid, (own, more) = self.grid, self.state
            ka, sa = halves(own[0], more[0], grid.x)
            kb, sb = halves(own[1], more[1], grid.y)
            self.state = (ka, grid.over_x(sa), kb, grid.over_y(sb))

    def second(self):
        if self.staged:
            grid, (ka, ma, kb, mb) = self.grid, self.state
            ka, sa = halves(ka, ma, grid.y)
            kb, sb = halves(kb, mb, grid.x)
            self.state = (ka, grid.over_y(sa), kb, grid.over_x(sb))

    def far_z(self):
        if self.staged:
            low, (ka, ma, kb, mb) = self.grid.z < 2, self.state
            a, b = both(ka, ma), both(kb, mb)
            self.state = (jnp.where(low, a, b), self.grid.flip_z(jnp.where(low, b, a), 2))

    def near_z(self):
        if self.staged:
            keep, send = halves(*self.state, self.grid.z % 2)
            self.state = (keep, self.grid.flip_z(send, 1))

    def along_z(self):
        if self.staged:
            z, (ka, ma, kb, mb) = self.grid.z, self.state
            last = jnp.concatenate([both(ka, ma), both(kb, mb)])
            self.state = (pick(last, z, 0),) + tuple(
                self.grid.over_z(pick(last, (z + shift) % 4, 0), shift) for shift in (1, 2, 3)
            )

    def result(self):
        if not self.staged:
            return lax.psum_scatter(self.state, AXES, scatter_dimension=0, tiled=True)
        total = self.state[0].astype(f32)
        for more in self.state[1:]:
            total = total + more.astype(f32)
        return total


class SumVectors:
    def __init__(self, grid, packed):
        self.grid, self.staged = grid, grid.nz == 4 and grid.ny == 2
        self.state = packed if self.staged else lax.psum(packed, AXES)

    def add(self, over):
        if self.staged:
            self.state = self.state + over(self.state)


def layer_norm(values, gain, shift):
    mean = jnp.mean(values, axis=-1, keepdims=True)
    centered = values - mean
    spread = jnp.mean(centered * centered, axis=-1, keepdims=True)
    return centered * lax.rsqrt(spread + eps) * gain + shift


def norm_back(values, gain, shift, upstream):
    result, pull = jax.vjp(layer_norm, values, gain, shift)
    return pull(upstream)


def smooth_gate(values):
    return jax.nn.gelu(values, approximate=True)


def by_rows(a, b):
    return lax.dot_general(a, b, (((1,), (1,)), ((), ())), preferred_element_type=f32)


def by_columns(a, b):
    return lax.dot_general(a, b, (((0,), (0,)), ((), ())), preferred_element_type=f32)


def fill(info, own, other, whole, block):
    for j in range(2):
        rows = slice(j * block, (j + 1) * block)
        whole[pl.ds(pl.multiple_of(info[j] * block, block), block), :] = own[rows, :]
        whole[pl.ds(pl.multiple_of(info[2 + j] * block, block), block), :] = other[rows, :]


def head_part(values, h):
    lane = lax.broadcasted_iota(jnp.int32, values.shape, 1)
    return jnp.where(lane // DH == h, values, jnp.zeros_like(values))


def keep_mask(starts, index, first, keys, block):
    key_pos = lax.broadcasted_iota(jnp.int32, (keys, block), 0)
    query_pos = first + lax.broadcasted_iota(jnp.int32, (1, block), 1)
    start = starts[pl.ds(index, 1), :]
    return (key_pos >= start) & (key_pos <= query_pos)


def attend_kernel(block, info, starts, q, k, v, ko, vo, out, lse, kn, vn):
    fill(info, k, ko, kn, block)
    fill(info, v, vo, vn, block)

    def run(index, count):
        at = pl.ds(pl.multiple_of(index * block, block), block)
        keys, vals = kn[: count * block, :], vn[: count * block, :]
        query = q[at, :] * jnp.asarray(DH**-0.5, bf16)
        keep = keep_mask(starts, index, info[index] * block, count * block, block)
        sides = []
        for h in range(2):
            scores = jnp.where(keep, by_rows(keys, head_part(query, h)), masked_value)
            top = jnp.max(scores, axis=0, keepdims=True)
            expo = jnp.exp(scores - top)
            total = jnp.sum(expo, axis=0, keepdims=True)
            lse[0, pl.ds(2 * h + index, 1), :] = top + jnp.log(total)
            side = by_columns(vals, expo.astype(bf16)) / total
            sides.append(side[h * DH : (h + 1) * DH])
        out[at, :] = jnp.concatenate(sides, axis=0).T.astype(bf16)

    low = info[4]
    for index, counts in ((low, (1, 2)), (1 - low, (3, 4))):
        for count in counts:
            pl.when(info[index] == count - 1)(functools.partial(run, index, count))


def attend_back_kernel(
    block, info, starts, q, k, v, ko, vo, out, lse, grad, dq, dkv, dkvo, kn, vn, dkn, dvn
):
    fill(info, k, ko, kn, block)
    fill(info, v, vo, vn, block)
    dkn[...] = jnp.zeros_like(dkn)
    dvn[...] = jnp.zeros_like(dvn)

    def run(index, count):
        at = pl.ds(pl.multiple_of(index * block, block), block)
        keys, vals = kn[: count * block, :], vn[: count * block, :]
        query = q[at, :] * jnp.asarray(DH**-0.5, bf16)
        up = grad[at, :]
        product = (up.astype(f32) * out[at, :].astype(f32)).T
        keep = keep_mask(starts, index, info[index] * block, count * block, block)
        sides = []
        for h in range(2):
            query_h, up_h = head_part(query, h), head_part(up, h)
            inner = jnp.sum(product[h * DH : (h + 1) * DH], axis=0, keepdims=True)
            scores = jnp.where(keep, by_rows(keys, query_h), masked_value)
            probs = jnp.exp(scores - lse[0, pl.ds(2 * h + index, 1), :])
            grad_scores = (probs * (by_rows(vals, up_h) - inner)).astype(bf16)
            dvn[: count * block, :] += jnp.dot(
                probs.astype(bf16), up_h, preferred_element_type=f32
            )
            dkn[: count * block, :] += jnp.dot(grad_scores, query_h, preferred_element_type=f32)
            side = by_columns(keys, grad_scores) * DH**-0.5
            sides.append(side[h * DH : (h + 1) * DH])
        dq[at, :] = jnp.concatenate(sides, axis=0).T.astype(bf16)

    low = info[4]
    for index, counts in ((low, (1, 2)), (1 - low, (3, 4))):
        for count in counts:
            pl.when(info[index] == count - 1)(functools.partial(run, index, count))
    for j in range(2):
        rows = slice(j * block, (j + 1) * block)
        own = pl.ds(pl.multiple_of(info[j] * block, block), block)
        other = pl.ds(pl.multiple_of(info[2 + j] * block, block), block)
        for i, whole in enumerate((dkn, dvn)):
            dkv[i, rows, :] = whole[own, :]
            dkvo[i, rows, :] = whole[other, :].astype(bf16)


def attend_specs(count, width, at):
    pairs = width // PAIR
    return [
        pl.BlockSpec((2, count // 2), lambda h, info: (0, 0)),
        pl.BlockSpec((count, PAIR), lambda h, info: (0, at + h)),
        pl.BlockSpec((count, PAIR), lambda h, info: (0, pairs + at + h)),
        pl.BlockSpec((count, PAIR), lambda h, info: (0, 2 * pairs + at + h)),
        pl.BlockSpec((count, PAIR), lambda h, info: (0, at + h)),
        pl.BlockSpec((count, PAIR), lambda h, info: (0, pairs + at + h)),
    ]


def attend(info, starts, mixed, other, part, parts):
    count, width = mixed.shape[0], mixed.shape[1] // 3
    pairs, block = width // PAIR // parts, count // 2
    column = pl.BlockSpec((count, PAIR), lambda h, info: (0, h))
    return pl.pallas_call(
        functools.partial(attend_kernel, block),
        out_shape=(
            jax.ShapeDtypeStruct((count, width // parts), bf16),
            jax.ShapeDtypeStruct((pairs, 4, block), f32),
        ),
        grid_spec=pltpu.PrefetchScalarGridSpec(
            num_scalar_prefetch=1,
            grid=(pairs,),
            in_specs=attend_specs(count, width, part * pairs),
            out_specs=[column, pl.BlockSpec((1, 4, block), lambda h, info: (h, 0, 0))],
            scratch_shapes=[pltpu.VMEM((2 * count, PAIR), bf16)] * 2,
        ),
        compiler_params=pltpu.CompilerParams(vmem_limit_bytes=32 * 2**20),
        cost_estimate=pl.CostEstimate(
            flops=8 * count * count * width // parts, bytes_accessed=12 * count * width // parts,
            transcendentals=20 * count * count // parts,
        ),
        name="attend",
    )(info, starts, mixed, mixed, mixed, other, other)


def attend_back(info, starts, mixed, other, attended, lse, grad, part, parts):
    count, width = grad.shape
    pairs, block = width // PAIR // parts, count // 2
    column = pl.BlockSpec((count, PAIR), lambda h, info: (0, h))
    return pl.pallas_call(
        functools.partial(attend_back_kernel, block),
        out_shape=(
            jax.ShapeDtypeStruct((count, width // parts), bf16),
            jax.ShapeDtypeStruct((2, count, width // parts), f32),
            jax.ShapeDtypeStruct((2, count, width // parts), bf16),
        ),
        grid_spec=pltpu.PrefetchScalarGridSpec(
            num_scalar_prefetch=1,
            grid=(pairs,),
            in_specs=attend_specs(count, width, part * pairs)
            + [
                column,
                pl.BlockSpec((1, 4, block), lambda h, info: (h, 0, 0)),
                pl.BlockSpec((count, PAIR), lambda h, info: (0, part * pairs + h)),
            ],
            out_specs=[column] + [pl.BlockSpec((2, count, PAIR), lambda h, info: (0, 0, h))] * 2,
            scratch_shapes=[pltpu.VMEM((2 * count, PAIR), bf16)] * 2
            + [pltpu.VMEM((2 * count, PAIR), f32)] * 2,
        ),
        compiler_params=pltpu.CompilerParams(vmem_limit_bytes=32 * 2**20),
        cost_estimate=pl.CostEstimate(
            flops=20 * count * count * width // parts, bytes_accessed=28 * count * width // parts,
            transcendentals=20 * count * count // parts,
        ),
        name="attend_back",
    )(info, starts, mixed, mixed, mixed, other, other, attended, lse, grad)


def local(
    n_fsdp,
    n_tok,
    tokens,
    cotangent,
    doc_lengths,
    norm1_gain,
    norm1_shift,
    w_qkv,
    bias_query,
    bias_value,
    w_out,
    bias_out,
    norm2_gain,
    norm2_shift,
    w_fc1,
    bias_fc1,
    w_fc2,
    bias_fc2,
):
    grid = Grid(n_fsdp, n_tok)
    y, t = grid.y, grid.t
    block, width = tokens.shape[2:]
    hidden_width = w_fc1.shape[1]

    def swap(values):
        mine, theirs = pick(values, y, 0)[0], pick(values, 1 - y, 0)[0]
        return jnp.concatenate([mine, grid.over_yc(theirs)], axis=0)

    def swap_back(values):
        mine, back = values[:block], grid.over_yc(values[block:])
        first, second = jnp.where(y == 0, mine, back), jnp.where(y == 0, back, mine)
        return jnp.stack([first, second])[:, None]

    live = {}
    kinds = (Gather, Scatter, GatherVectors, SumVectors)

    def step(*names):
        moving = [live[n].state if isinstance(live[n], kinds) else live[n] for n in names]
        for name, value in zip(names, lax.optimization_barrier(moving)):
            if isinstance(live[name], kinds):
                live[name].state = value
            else:
                live[name] = value

    vectors = (
        norm1_gain, norm1_shift, bias_query, bias_value, bias_out, norm2_gain, norm2_shift, bias_fc2
    )
    part = norm1_gain.shape[0]
    packed = jnp.concatenate([v[None] for v in vectors] + [bias_fc1.reshape(-1, part)], axis=0)
    w1, w2, w3, small = (
        Gather(grid, w_qkv), Gather(grid, w_out, w_fc1), Gather(grid, w_fc2), GatherVectors(grid, packed)
    )
    live.update(w1=w1, w2=w2, w3=w3, small=small)

    mine, across = jnp.stack([t, 3 - t]), jnp.stack([t ^ 1, 3 - (t ^ 1)])
    info = jnp.concatenate([mine, across, y[None]]).astype(jnp.int32)
    lengths = pick(doc_lengths, y, 0)[0]
    ends = jnp.cumsum(lengths)
    place = mine[:, None] * block + jnp.arange(block, dtype=jnp.int32)[None]
    starts = jnp.max(
        jnp.where(place[..., None] >= ends, ends, 0), axis=-1
    ).astype(jnp.int32)

    w1.along_z()
    live["rows"] = swap(tokens)
    small.over_x()
    step("w1", "rows", "small", "w2")
    w1.first()
    w2.near_z()
    small.over_z(1)
    step("w1", "w2", "small")
    w1.second()
    w2.far_z()
    small.over_z(2)
    step("w1", "small", "w3")
    w1.last()
    w3.near_z()
    live["up"] = swap(cotangent)
    packed = small.state
    gain1, shift1, b_query, b_value, b_out, gain2, shift2, b_fc2 = (
        packed[:, i].reshape(width).astype(f32) for i in range(8)
    )
    b_fc1 = packed[:, 8:].reshape(hidden_width).astype(f32)
    inputs = live["rows"].astype(f32)
    live["normed"] = layer_norm(inputs, gain1, shift1).astype(bf16)
    step("w1", "w2", "w3", "normed", "up")
    w2.first()
    (full_qkv,) = w1.place()
    b_qkv = jnp.concatenate([b_query, jnp.zeros_like(b_query), b_value])
    normed = live["normed"]
    live["mixed"] = (jnp.dot(normed, full_qkv, preferred_element_type=f32) + b_qkv).astype(bf16)
    step("mixed", "w3")
    w3.far_z()
    live["other"] = grid.over_core(live["mixed"][:, width:])
    step("mixed", "other")
    low, low_lse = attend(info, starts, live["mixed"], live["other"], 0, 2)
    live["low"] = low
    step("low", "other", "mixed", "w2")
    w2.second()
    high, high_lse = attend(info, starts, live["mixed"], live["other"], 1, 2)
    live["high"] = high
    step("high", "w2", "w3")
    w2.last()
    w3.first()
    attended = jnp.concatenate([live["low"], live["high"]], axis=1)
    live["attended"] = attended
    step("w2", "attended")
    attended = live["attended"]
    full_out, full_fc1 = w2.place()
    middle = inputs + jnp.dot(attended, full_out, preferred_element_type=f32) + b_out
    live["middle"] = middle
    live["normed2"] = layer_norm(middle, gain2, shift2).astype(bf16)
    live["hidden"] = jnp.dot(live["normed2"], full_fc1, preferred_element_type=f32) + b_fc1
    step("hidden", "normed2", "middle", "w3")
    w3.second()
    normed2, middle, upstream = live["normed2"], live["middle"], live["up"]
    live["active"] = smooth_gate(live["hidden"]).astype(bf16)
    live["fc2"] = Scatter(grid, live["active"], upstream)
    step("fc2", "active", "hidden", "w3")

    w3.last()
    live["fc2"].core()
    step("w3", "fc2", "hidden")
    live["fc2"].first()
    (full_fc2,) = w3.place()
    grad_out = upstream.astype(f32)
    grad_bias_fc2 = jnp.sum(grad_out, axis=0)
    unused, gate_pull = jax.vjp(smooth_gate, live["hidden"])
    grad_hidden = gate_pull(by_rows(upstream, full_fc2))[0].astype(bf16)
    live["grad_hidden"] = grad_hidden
    grad_bias_fc1 = jnp.sum(grad_hidden.astype(f32), axis=0)
    step("grad_hidden")
    grad_hidden = live["grad_hidden"]
    live["fc1"] = Scatter(grid, normed2, grad_hidden)
    step("fc1", "grad_hidden", "fc2")
    live["fc2"].second()
    live["fc1"].core()
    live["up2"] = by_rows(live["grad_hidden"], full_fc1)
    step("fc1", "up2")
    grad_mid_norm, grad_gain2, grad_shift2 = norm_back(middle, gain2, shift2, live["up2"])
    grad_middle = grad_out + grad_mid_norm
    grad_branch = grad_middle.astype(bf16)
    grad_bias_out = jnp.sum(grad_branch.astype(f32), axis=0)
    live["grad_attended"] = by_rows(grad_branch, full_out).astype(bf16)
    live["out"] = Scatter(grid, attended, grad_branch)
    step("grad_attended", "out", "fc1", "fc2")
    live["fc2"].far_z()
    live["fc1"].first()
    live["out"].core()
    parts = [
        attend_back(
            info, starts, live["mixed"], live["other"], live["low"], low_lse,
            live["grad_attended"], 0, 2,
        )
    ]
    live["part"] = parts[0]
    step("part", "grad_attended", "out", "fc1", "fc2")
    parts[0] = live["part"]
    live["fc2"].near_z()
    live["fc1"].second()
    live["back"] = grid.over_core(parts[0][2])
    parts.append(
        attend_back(
            info, starts, live["mixed"], live["other"], live["high"], high_lse,
            live["grad_attended"], 1, 2,
        )
    )
    live["part"] = parts[1]
    step("part", "back", "fc1", "fc2", "out", "active")
    parts[1] = live["part"]
    live["fc1"].far_z()
    live["out"].first()
    live["back2"] = grid.over_core(parts[1][2])
    result = middle + jnp.dot(live["active"], full_fc2, preferred_element_type=f32) + b_fc2
    live["output"] = result.astype(bf16)
    step("back", "back2", "output", "out")
    live["out"].second()
    output = swap_back(live["output"])
    dkv = [both(p[1], live[n]) for p, n in zip(parts, ("back", "back2"))]
    grad_mixed = jnp.concatenate(
        [p[0] for p in parts] + [d[0] for d in dkv] + [d[1] for d in dkv], axis=1
    )
    live["grad_mixed"] = grad_mixed
    live["qkv"] = Scatter(grid, normed, grad_mixed)
    step("qkv", "grad_mixed", "fc1", "out")
    live["qkv"].core()
    live["fc1"].near_z()
    live["out"].far_z()
    grad_mixed = live["grad_mixed"]
    live["up1"] = by_rows(grad_mixed, full_qkv)
    step("qkv", "up1", "grad_mixed", "out")
    live["qkv"].first()
    live["out"].near_z()
    grad_mixed = live["grad_mixed"]
    grad_bias_query = jnp.sum(grad_mixed[:, :width].astype(f32), axis=0)
    grad_bias_value = jnp.sum(grad_mixed[:, 2 * width :].astype(f32), axis=0)
    grad_in_norm, grad_gain1, grad_shift1 = norm_back(inputs, gain1, shift1, live["up1"])
    live["grad_tokens"] = (grad_middle + grad_in_norm).astype(bf16)
    sums = SumVectors(
        grid,
        jnp.concatenate(
            [
                v.reshape(-1, width)
                for v in (
                    grad_gain1, grad_shift1, grad_bias_query, grad_bias_value, grad_bias_out,
                    grad_gain2, grad_shift2, grad_bias_fc2, grad_bias_fc1,
                )
            ],
            axis=0,
        ),
    )
    live["sums"] = sums
    step("sums", "grad_tokens", "out")
    grad_tokens = swap_back(live["grad_tokens"])
    sums.add(grid.over_core)
    sums.add(grid.over_x)
    step("sums", "qkv")
    live["qkv"].second()
    sums.add(grid.over_y)
    step("sums", "qkv")
    live["qkv"].along_z()
    sums.add(lambda v: grid.flip_z(v, 1))
    sums.add(lambda v: grid.flip_z(v, 2))
    sums = sums.state
    grad_qkv, grad_w_out, grad_fc1, grad_fc2 = (
        live[n].result() for n in ("qkv", "out", "fc1", "fc2")
    )

    device, devices = grid.f * n_tok + t, n_fsdp * n_tok

    def owned(vector):
        count = vector.shape[0] // devices
        return lax.dynamic_slice_in_dim(vector, device * count, count, 0)

    return (
        output,
        grad_tokens,
        owned(sums[0]),
        owned(sums[1]),
        grad_qkv,
        owned(sums[2]),
        owned(sums[3]),
        grad_w_out,
        owned(sums[4]),
        owned(sums[5]),
        owned(sums[6]),
        grad_fc1,
        owned(sums[8:].reshape(hidden_width)),
        grad_fc2,
        owned(sums[7]),
    )


def solution(mesh):
    vector, matrix = P("fsdp"), P("fsdp", None)
    rows = P(None, "fsdp", "tok", None)
    own_vector, own_matrix = P(("fsdp", "tok")), P(("fsdp", "tok"), None)
    return jax.shard_map(
        functools.partial(local, mesh.shape["fsdp"], mesh.shape["tok"]),
        mesh=mesh,
        in_specs=(
            rows, rows, P(None, "fsdp", None), vector, vector, matrix, vector, vector,
            matrix, vector, vector, vector, matrix, vector, matrix, vector,
        ),
        out_specs=(
            rows, rows, own_vector, own_vector, own_matrix, own_vector, own_vector,
            own_matrix, own_vector, own_vector, own_vector, own_matrix, own_vector,
            own_matrix, own_vector,
        ),
        check_vma=False,
    )
```

```python
import functools

import jax
import jax.numpy as jnp
from jax import lax
from jax.experimental import pallas as pl
from jax.experimental.pallas import tpu as pltpu
from jax.sharding import PartitionSpec as P

DH = 64
PAIR = 2 * DH
eps = 1e-05
masked_value = -1e30
f32 = jnp.float32
bf16 = jnp.bfloat16
AXES = ("fsdp", "tok")


class Grid:
    def __init__(self, n_fsdp, n_tok):
        self.n_fsdp, self.n_tok = n_fsdp, n_tok
        self.nz, self.ny = n_fsdp // 2, n_tok // 2
        self.f, self.t = lax.axis_index("fsdp"), lax.axis_index("tok")
        self.z, self.x = self.f // 2, self.f % 2
        self.y, self.c = self.t // 2, self.t % 2

    def staged(self, rows):
        return self.nz == 4 and self.ny == 2 and rows % 16 == 0

    def send(self, value, place):
        pairs = []
        for f in range(self.n_fsdp):
            for t in range(self.n_tok):
                z, x, y, c = place(f // 2, f % 2, t // 2, t % 2)
                pairs.append((f * self.n_tok + t, (z * 2 + x) * self.n_tok + y * 2 + c))
        return lax.ppermute(value, AXES, pairs)

    def over_core(self, value):
        return self.send(value, lambda z, x, y, c: (z, x, y, 1 - c))

    def over_x(self, value):
        return self.send(value, lambda z, x, y, c: (z, 1 - x, y, c))

    def over_y(self, value):
        return self.send(value, lambda z, x, y, c: (z, x, 1 - y, c))

    def over_yc(self, value):
        return self.send(value, lambda z, x, y, c: (z, x, 1 - y, 1 - c))

    def flip_z(self, value, bit):
        return self.send(value, lambda z, x, y, c: (z ^ bit, x, y, c))

    def over_z(self, value, shift):
        return self.send(value, lambda z, x, y, c: ((z + shift) % self.nz, x, y, c))


def pick(values, index, axis):
    return lax.dynamic_index_in_dim(values, index, axis, keepdims=False)


def both(a, b):
    return (a.astype(f32) + b.astype(f32)).astype(bf16)


def halves(a, b, index, lead=()):
    def part(values, i):
        rest = values.shape[len(lead) + 1 :]
        start = lead + (i,) + (0,) * len(rest)
        return lax.dynamic_slice(values, start, (1,) * (len(lead) + 1) + rest).reshape(rest)

    return both(part(a, index), part(b, index)), both(part(a, 1 - index), part(b, 1 - index))


def place_kernel(rows, widths, offsets, *refs):
    sem, outs, pieces = refs[-1], refs[-1 - len(widths) : -1], refs[: -1 - len(widths)]
    copies = []
    at = 0
    for piece in pieces:
        for j in range(piece.shape[0]):
            first = pl.multiple_of(offsets[at], rows)
            column = 0
            for i, width in enumerate(widths):
                copies.append(
                    pltpu.make_async_copy(
                        piece.at[j, :, pl.ds(column, width)],
                        outs[i].at[pl.ds(first, rows)],
                        sem.at[at * len(widths) + i],
                    )
                )
                column += width
            at += 1
    for copy in copies:
        copy.start()
    for copy in copies:
        copy.wait()


class Gather:
    def __init__(self, grid, *shards):
        self.grid, self.shards = grid, shards
        self.rows = shards[0].shape[0] // grid.n_tok
        self.staged = grid.staged(self.rows)
        self.state = {"shards": list(shards)}
        self.flip = True

    def own(self):
        parts = [
            lax.dynamic_slice_in_dim(w, self.grid.t * self.rows, self.rows, 0)
            for w in self.state["shards"]
        ]
        return jnp.concatenate(parts, axis=1)

    def along_z(self):
        if self.staged:
            own = self.own()
            self.flip = False
            self.state = {"steps": [own] + [self.grid.over_z(own, k) for k in (1, 2, 3)]}

    def beside_z(self):
        if self.staged:
            own = self.own()
            self.flip = False
            self.state = {"own": own, "z1": self.grid.over_z(own, 1), "z3": self.grid.over_z(own, 3)}

    def across_z(self):
        if self.staged:
            state = self.state
            self.state = {
                "steps": [state["own"], state["z1"], self.grid.over_z(state["own"], 2), state["z3"]]
            }

    def near_z(self):
        if self.staged:
            own = self.own()
            self.state = {"steps": [own, self.grid.flip_z(own, 1)]}

    def far_z(self):
        if self.staged:
            two = jnp.stack(self.state["steps"])
            self.state = {"steps": [two, self.grid.flip_z(two, 2)]}

    def first(self):
        if self.staged:
            grid, steps = self.grid, self.state["steps"]
            q = jnp.concatenate(steps) if self.flip else jnp.stack(steps)
            self.state = {"q": q, "x": [grid.over_x(q[:2])], "y": [grid.over_y(q[2:])]}

    def first_whole(self):
        if self.staged:
            grid, q = self.grid, jnp.stack(self.state["steps"])
            self.state = {"q": q, "x": [grid.over_x(q)], "y": [grid.over_y(q)]}

    def first_rest(self):
        if self.staged:
            grid, state = self.grid, self.state
            state["x"] = state["x"] + [grid.over_x(state["q"][2:])]
            state["y"] = [grid.over_y(state["q"][:2])] + state["y"]

    def second(self):
        if self.staged:
            state, grid = self.state, self.grid
            state["a"] = grid.over_y(state["x"][0][:2])
            state["b"] = grid.over_x(state["y"][-1][-2:])
            state["near"] = grid.over_core(
                jnp.concatenate([state["q"]] + state["x"] + state["y"])
            )

    def last(self):
        if self.staged:
            state = self.state
            state["cab"] = self.grid.over_core(jnp.concatenate([state["a"], state["b"]]))

    def place(self):
        if not self.staged:
            return [lax.all_gather(w, "fsdp", axis=0, tiled=True) for w in self.state["shards"]]
        grid, rows = self.grid, self.rows
        shard_rows, kind = self.shards[0].shape[0], self.shards[0].dtype
        widths = [w.shape[1] for w in self.shards]
        at = lambda dx, dy: [(k, dx, dy) for k in range(4)]
        ab = at(1, 1)
        order = (
            ("q", at(0, 0), 0), ("x", at(1, 0), 0), ("y", at(0, 1), 0), ("a", ab[:2], 0),
            ("b", ab[2:], 0), ("near", at(0, 0) + at(1, 0) + at(0, 1), 1), ("cab", ab, 1),
        )
        offsets, pieces = [], []
        for name, places, dc in order:
            have = self.state[name]
            pieces += have if isinstance(have, (list, tuple)) else [have]
            for k, dx, dy in places:
                z = grid.z ^ k if self.flip else (grid.z + 4 - k) % 4
                x, y, c = grid.x ^ dx, grid.y ^ dy, grid.c ^ dc
                offsets.append((z * 2 + x) * shard_rows + (y * 2 + c) * rows)
        total = grid.n_fsdp * shard_rows
        return pl.pallas_call(
            functools.partial(place_kernel, rows, widths),
            out_shape=[jax.ShapeDtypeStruct((total, width), kind) for width in widths],
            in_specs=[pl.BlockSpec(memory_space=pltpu.SMEM)]
            + [pl.BlockSpec(memory_space=pl.ANY)] * len(pieces),
            out_specs=[pl.BlockSpec(memory_space=pltpu.VMEM)] * len(widths),
            scratch_shapes=[pltpu.SemaphoreType.DMA((len(offsets) * len(widths),))],
            compiler_params=pltpu.CompilerParams(vmem_limit_bytes=24 * 2**20),
            cost_estimate=pl.CostEstimate(
                flops=0, bytes_accessed=4 * total * sum(widths), transcendentals=0
            ),
            name="place",
        )(jnp.stack(offsets).astype(jnp.int32), *pieces)


class GatherVectors:
    def __init__(self, grid, packed):
        self.grid, self.staged = grid, grid.nz == 4
        self.state = packed

    def over_x(self):
        if not self.staged:
            self.state = lax.all_gather(self.state, "fsdp", axis=0)
            return
        whole = jnp.zeros((self.grid.n_fsdp,) + self.state.shape, self.state.dtype)
        whole = lax.dynamic_update_index_in_dim(whole, self.state, self.grid.f, 0)
        self.state = whole + self.grid.over_x(whole)

    def over_z(self, bit):
        if self.staged:
            self.state = self.state + self.grid.flip_z(self.state, bit)


def split_kernel(rows, core, left, right, own, other, turned):
    @pl.when(pl.program_id(1) == 0)
    def turn():
        turned[...] = left[...].T

    total = jnp.dot(turned[...], right[...], preferred_element_type=f32).astype(bf16)
    first = core[0] == 0

    def put(order):
        for x in range(2):
            for y in range(2):
                at = (x * 2 + y) * 2 * rows
                low, high = total[at : at + rows], total[at + rows : at + 2 * rows]
                i, j = (x, y) if order else (y, x)
                own[0, i, j, 0] = jnp.where(first, low, high)
                other[0, i, j, 0] = jnp.where(first, high, low)

    z = pl.program_id(0)
    pl.when(z < 2)(lambda: put(True))
    pl.when(z >= 2)(lambda: put(False))


class Scatter:
    def __init__(self, grid, left, right):
        self.grid = grid
        count, height, width = left.shape + right.shape[1:]
        rows = height // (grid.n_fsdp * grid.n_tok)
        self.staged = grid.staged(rows)
        if not self.staged:
            self.state = by_columns(left, right)
            return
        tile = min(width, 1024 if rows <= 32 else 512)
        part = jax.ShapeDtypeStruct((2, 2, 2, 2, rows, width), bf16)
        block = pl.BlockSpec(
            (1, 2, 2, 1, rows, tile), lambda z, n, core: (z // 2, 0, 0, z % 2, 0, n)
        )
        self.state = pl.pallas_call(
            functools.partial(split_kernel, rows),
            out_shape=(part, part),
            grid_spec=pltpu.PrefetchScalarGridSpec(
                num_scalar_prefetch=1,
                grid=(4, width // tile),
                in_specs=[
                    pl.BlockSpec((count, 8 * rows), lambda z, n, core: (0, z)),
                    pl.BlockSpec((count, tile), lambda z, n, core: (0, n)),
                ],
                out_specs=[block, block],
                scratch_shapes=[pltpu.VMEM((8 * rows, count), bf16)],
            ),
            compiler_params=pltpu.CompilerParams(vmem_limit_bytes=32 * 2**20),
            cost_estimate=pl.CostEstimate(
                flops=2 * count * height * width,
                bytes_accessed=2 * (height * width + count * (height + width)),
                transcendentals=0,
            ),
            name="grad_split",
        )(grid.c[None].astype(jnp.int32), left, right)

    def core(self):
        if self.staged:
            own, other = self.state
            self.state = (own, self.grid.over_core(other))

    def first(self):
        if self.staged:
            grid, (own, more) = self.grid, self.state
            ka, sa = halves(own, more, grid.x, (0,))
            kb, sb = halves(own, more, grid.y, (1,))
            self.state = (ka, grid.over_x(sa), kb, grid.over_y(sb))

    def second(self):
        if self.staged:
            grid, (ka, ma, kb, mb) = self.grid, self.state
            ka, sa = halves(ka, ma, grid.y)
            kb, sb = halves(kb, mb, grid.x)
            self.state = (ka, grid.over_y(sa), kb, grid.over_x(sb))

    def far_z(self):
        if self.staged:
            low, (ka, ma, kb, mb) = self.grid.z < 2, self.state
            a, b = both(ka, ma), both(kb, mb)
            self.state = (jnp.where(low, a, b), self.grid.flip_z(jnp.where(low, b, a), 2))

    def near_z(self):
        if self.staged:
            keep, send = halves(*self.state, self.grid.z % 2)
            self.state = (keep, self.grid.flip_z(send, 1))

    def along_z(self):
        if self.staged:
            z, (ka, ma, kb, mb) = self.grid.z, self.state
            last = jnp.concatenate([both(ka, ma), both(kb, mb)])
            self.state = (pick(last, z, 0),) + tuple(
                self.grid.over_z(pick(last, (z + shift) % 4, 0), shift) for shift in (1, 2, 3)
            )

    def result(self):
        if not self.staged:
            return lax.psum_scatter(self.state, AXES, scatter_dimension=0, tiled=True)
        total = self.state[0].astype(f32)
        for more in self.state[1:]:
            total = total + more.astype(f32)
        return total


class SumVectors:
    def __init__(self, grid, packed):
        self.grid, self.staged = grid, grid.nz == 4 and grid.ny == 2
        self.state = packed if self.staged else lax.psum(packed, AXES)

    def add(self, over):
        if self.staged:
            self.state = self.state + over(self.state)


def layer_norm(values, gain, shift):
    mean = jnp.mean(values, axis=-1, keepdims=True)
    centered = values - mean
    spread = jnp.mean(centered * centered, axis=-1, keepdims=True)
    return centered * lax.rsqrt(spread + eps) * gain + shift


def norm_back(values, gain, shift, upstream):
    result, pull = jax.vjp(layer_norm, values, gain, shift)
    return pull(upstream)


def smooth_gate(values):
    return jax.nn.gelu(values, approximate=True)


def by_rows(a, b):
    return lax.dot_general(a, b, (((1,), (1,)), ((), ())), preferred_element_type=f32)


def by_columns(a, b):
    return lax.dot_general(a, b, (((0,), (0,)), ((), ())), preferred_element_type=f32)


def fill(info, own, other, whole, block):
    for j in range(2):
        rows = slice(j * block, (j + 1) * block)
        whole[pl.ds(pl.multiple_of(info[j] * block, block), block), :] = own[rows, :]
        whole[pl.ds(pl.multiple_of(info[2 + j] * block, block), block), :] = other[rows, :]


def head_part(values, h):
    lane = lax.broadcasted_iota(jnp.int32, values.shape, 1)
    return jnp.where(lane // DH == h, values, jnp.zeros_like(values))


def keep_mask(starts, index, first, keys, block):
    key_pos = lax.broadcasted_iota(jnp.int32, (keys, block), 0)
    query_pos = first + lax.broadcasted_iota(jnp.int32, (1, block), 1)
    start = starts[pl.ds(index, 1), :]
    return (key_pos >= start) & (key_pos <= query_pos)


def attend_kernel(block, info, starts, q, k, v, ko, vo, out, lse, kn, vn):
    fill(info, k, ko, kn, block)
    fill(info, v, vo, vn, block)

    def run(index, count):
        at = pl.ds(pl.multiple_of(index * block, block), block)
        keys, vals = kn[: count * block, :], vn[: count * block, :]
        query = q[at, :] * jnp.asarray(DH**-0.5, bf16)
        keep = keep_mask(starts, index, info[index] * block, count * block, block)
        sides = []
        for h in range(2):
            scores = jnp.where(keep, by_rows(keys, head_part(query, h)), masked_value)
            top = jnp.max(scores, axis=0, keepdims=True)
            expo = jnp.exp(scores - top)
            total = jnp.sum(expo, axis=0, keepdims=True)
            lse[0, pl.ds(2 * h + index, 1), :] = top + jnp.log(total)
            side = by_columns(vals, expo.astype(bf16)) / total
            sides.append(side[h * DH : (h + 1) * DH])
        out[at, :] = jnp.concatenate(sides, axis=0).T.astype(bf16)

    low = info[4]
    for index, counts in ((low, (1, 2)), (1 - low, (3, 4))):
        for count in counts:
            pl.when(info[index] == count - 1)(functools.partial(run, index, count))


def attend_back_kernel(
    block, info, starts, q, k, v, ko, vo, out, lse, grad, dq, dkv, dkvo, kn, vn, dkn, dvn
):
    fill(info, k, ko, kn, block)
    fill(info, v, vo, vn, block)
    dkn[...] = jnp.zeros_like(dkn)
    dvn[...] = jnp.zeros_like(dvn)

    def run(index, count):
        at = pl.ds(pl.multiple_of(index * block, block), block)
        keys, vals = kn[: count * block, :], vn[: count * block, :]
        query = q[at, :] * jnp.asarray(DH**-0.5, bf16)
        up = grad[at, :]
        product = (up.astype(f32) * out[at, :].astype(f32)).T
        keep = keep_mask(starts, index, info[index] * block, count * block, block)
        sides = []
        for h in range(2):
            query_h, up_h = head_part(query, h), head_part(up, h)
            inner = jnp.sum(product[h * DH : (h + 1) * DH], axis=0, keepdims=True)
            scores = jnp.where(keep, by_rows(keys, query_h), masked_value)
            probs = jnp.exp(scores - lse[0, pl.ds(2 * h + index, 1), :])
            grad_scores = (probs * (by_rows(vals, up_h) - inner)).astype(bf16)
            dvn[: count * block, :] += jnp.dot(
                probs.astype(bf16), up_h, preferred_element_type=f32
            )
            dkn[: count * block, :] += jnp.dot(grad_scores, query_h, preferred_element_type=f32)
            side = by_columns(keys, grad_scores) * DH**-0.5
            sides.append(side[h * DH : (h + 1) * DH])
        dq[at, :] = jnp.concatenate(sides, axis=0).T.astype(bf16)

    low = info[4]
    for index, counts in ((low, (1, 2)), (1 - low, (3, 4))):
        for count in counts:
            pl.when(info[index] == count - 1)(functools.partial(run, index, count))
    for j in range(2):
        rows = slice(j * block, (j + 1) * block)
        own = pl.ds(pl.multiple_of(info[j] * block, block), block)
        other = pl.ds(pl.multiple_of(info[2 + j] * block, block), block)
        for i, whole in enumerate((dkn, dvn)):
            dkv[i, rows, :] = whole[own, :]
            dkvo[i, rows, :] = whole[other, :].astype(bf16)


def attend_specs(count, width, at):
    pairs = width // PAIR
    return [
        pl.BlockSpec((2, count // 2), lambda h, info: (0, 0)),
        pl.BlockSpec((count, PAIR), lambda h, info: (0, at + h)),
        pl.BlockSpec((count, PAIR), lambda h, info: (0, pairs + at + h)),
        pl.BlockSpec((count, PAIR), lambda h, info: (0, 2 * pairs + at + h)),
        pl.BlockSpec((count, PAIR), lambda h, info: (0, at + h)),
        pl.BlockSpec((count, PAIR), lambda h, info: (0, pairs + at + h)),
    ]


def attend(info, starts, mixed, other, part, parts):
    count, width = mixed.shape[0], mixed.shape[1] // 3
    pairs, block = width // PAIR // parts, count // 2
    column = pl.BlockSpec((count, PAIR), lambda h, info: (0, h))
    return pl.pallas_call(
        functools.partial(attend_kernel, block),
        out_shape=(
            jax.ShapeDtypeStruct((count, width // parts), bf16),
            jax.ShapeDtypeStruct((pairs, 4, block), f32),
        ),
        grid_spec=pltpu.PrefetchScalarGridSpec(
            num_scalar_prefetch=1,
            grid=(pairs,),
            in_specs=attend_specs(count, width, part * pairs),
            out_specs=[column, pl.BlockSpec((1, 4, block), lambda h, info: (h, 0, 0))],
            scratch_shapes=[pltpu.VMEM((2 * count, PAIR), bf16)] * 2,
        ),
        compiler_params=pltpu.CompilerParams(vmem_limit_bytes=32 * 2**20),
        cost_estimate=pl.CostEstimate(
            flops=8 * count * count * width // parts, bytes_accessed=12 * count * width // parts,
            transcendentals=20 * count * count // parts,
        ),
        name="attend",
    )(info, starts, mixed, mixed, mixed, other, other)


def attend_back(info, starts, mixed, other, attended, lse, grad, part, parts):
    count, width = grad.shape
    pairs, block = width // PAIR // parts, count // 2
    column = pl.BlockSpec((count, PAIR), lambda h, info: (0, h))
    return pl.pallas_call(
        functools.partial(attend_back_kernel, block),
        out_shape=(
            jax.ShapeDtypeStruct((count, width // parts), bf16),
            jax.ShapeDtypeStruct((2, count, width // parts), f32),
            jax.ShapeDtypeStruct((2, count, width // parts), bf16),
        ),
        grid_spec=pltpu.PrefetchScalarGridSpec(
            num_scalar_prefetch=1,
            grid=(pairs,),
            in_specs=attend_specs(count, width, part * pairs)
            + [
                column,
                pl.BlockSpec((1, 4, block), lambda h, info: (h, 0, 0)),
                pl.BlockSpec((count, PAIR), lambda h, info: (0, part * pairs + h)),
            ],
            out_specs=[column] + [pl.BlockSpec((2, count, PAIR), lambda h, info: (0, 0, h))] * 2,
            scratch_shapes=[pltpu.VMEM((2 * count, PAIR), bf16)] * 2
            + [pltpu.VMEM((2 * count, PAIR), f32)] * 2,
        ),
        compiler_params=pltpu.CompilerParams(vmem_limit_bytes=32 * 2**20),
        cost_estimate=pl.CostEstimate(
            flops=20 * count * count * width // parts, bytes_accessed=28 * count * width // parts,
            transcendentals=20 * count * count // parts,
        ),
        name="attend_back",
    )(info, starts, mixed, mixed, mixed, other, other, attended, lse, grad)


def local(
    n_fsdp,
    n_tok,
    tokens,
    cotangent,
    doc_lengths,
    norm1_gain,
    norm1_shift,
    w_qkv,
    bias_query,
    bias_value,
    w_out,
    bias_out,
    norm2_gain,
    norm2_shift,
    w_fc1,
    bias_fc1,
    w_fc2,
    bias_fc2,
):
    grid = Grid(n_fsdp, n_tok)
    y, t = grid.y, grid.t
    block, width = tokens.shape[2:]
    hidden_width = w_fc1.shape[1]

    def swap(values):
        mine, theirs = pick(values, y, 0)[0], pick(values, 1 - y, 0)[0]
        return jnp.concatenate([mine, grid.over_yc(theirs)], axis=0)

    def swap_back(values):
        mine, back = values[:block], grid.over_yc(values[block:])
        first, second = jnp.where(y == 0, mine, back), jnp.where(y == 0, back, mine)
        return jnp.stack([first, second])[:, None]

    live = {}
    kinds = (Gather, Scatter, GatherVectors, SumVectors)

    def step(*names):
        moving = [live[n].state if isinstance(live[n], kinds) else live[n] for n in names]
        for name, value in zip(names, lax.optimization_barrier(moving)):
            if isinstance(live[name], kinds):
                live[name].state = value
            else:
                live[name] = value

    vectors = (
        norm1_gain, norm1_shift, bias_query, bias_value, bias_out, norm2_gain, norm2_shift, bias_fc2
    )
    part = norm1_gain.shape[0]
    packed = jnp.concatenate([v[None] for v in vectors] + [bias_fc1.reshape(-1, part)], axis=0)
    w1, w2, w3, small = (
        Gather(grid, w_qkv), Gather(grid, w_out, w_fc1), Gather(grid, w_fc2), GatherVectors(grid, packed)
    )
    live.update(w1=w1, w2=w2, w3=w3, small=small)

    mine, across = jnp.stack([t, 3 - t]), jnp.stack([t ^ 1, 3 - (t ^ 1)])
    info = jnp.concatenate([mine, across, y[None]]).astype(jnp.int32)
    lengths = pick(doc_lengths, y, 0)[0]
    ends = jnp.cumsum(lengths)
    place = mine[:, None] * block + jnp.arange(block, dtype=jnp.int32)[None]
    starts = jnp.max(
        jnp.where(place[..., None] >= ends, ends, 0), axis=-1
    ).astype(jnp.int32)

    w1.along_z()
    live["rows"], live["up"] = swap(tokens), swap(cotangent)
    step("w1", "rows", "up", "small", "w2")
    w1.first_whole()
    w2.beside_z()
    small.over_x()
    step("w1", "w2", "small")
    w1.second()
    w2.across_z()
    small.over_z(1)
    step("w1", "w2", "small", "w3")
    w1.last()
    w2.first()
    small.over_z(2)
    packed = small.state
    gain1, shift1, b_query, b_value, b_out, gain2, shift2, b_fc2 = (
        packed[:, i].reshape(width).astype(f32) for i in range(8)
    )
    b_fc1 = packed[:, 8:].reshape(hidden_width).astype(f32)
    inputs = live["rows"].astype(f32)
    live["normed"] = layer_norm(inputs, gain1, shift1).astype(bf16)
    step("w1", "normed", "w3")
    w3.near_z()
    (full_qkv,) = w1.place()
    b_qkv = jnp.concatenate([b_query, jnp.zeros_like(b_query), b_value])
    normed = live["normed"]
    live["mixed"] = (jnp.dot(normed, full_qkv, preferred_element_type=f32) + b_qkv).astype(bf16)
    step("mixed", "w3", "w2")
    w2.first_rest()
    live["other"] = grid.over_core(live["mixed"][:, width:])
    step("mixed", "other")
    w3.far_z()
    low, low_lse = attend(info, starts, live["mixed"], live["other"], 0, 2)
    live["low"] = low
    step("low", "other", "mixed", "w2")
    w2.second()
    high, high_lse = attend(info, starts, live["mixed"], live["other"], 1, 2)
    live["high"] = high
    step("high", "w2", "w3")
    w2.last()
    w3.first()
    attended = jnp.concatenate([live["low"], live["high"]], axis=1)
    live["attended"] = attended
    step("w2", "attended")
    attended = live["attended"]
    full_out, full_fc1 = w2.place()
    middle = inputs + jnp.dot(attended, full_out, preferred_element_type=f32) + b_out
    live["middle"] = middle
    live["normed2"] = layer_norm(middle, gain2, shift2).astype(bf16)
    live["hidden"] = jnp.dot(live["normed2"], full_fc1, preferred_element_type=f32) + b_fc1
    step("hidden", "normed2", "middle", "w3")
    w3.first_rest()
    normed2, middle, upstream = live["normed2"], live["middle"], live["up"]
    live["active"] = smooth_gate(live["hidden"]).astype(bf16)
    live["fc2"] = Scatter(grid, live["active"], upstream)
    step("fc2", "active", "hidden", "w3")
    w3.second()
    live["fc2"].core()
    step("fc2", "hidden", "w3")

    w3.last()
    step("w3", "hidden")
    live["fc2"].first()
    (full_fc2,) = w3.place()
    grad_out = upstream.astype(f32)
    grad_bias_fc2 = jnp.sum(grad_out, axis=0)
    unused, gate_pull = jax.vjp(smooth_gate, live["hidden"])
    grad_hidden = gate_pull(by_rows(upstream, full_fc2))[0].astype(bf16)
    live["grad_hidden"] = grad_hidden
    grad_bias_fc1 = jnp.sum(grad_hidden.astype(f32), axis=0)
    step("grad_hidden", "fc2")
    live["fc2"].second()
    grad_hidden = live["grad_hidden"]
    live["fc1"] = Scatter(grid, normed2, grad_hidden)
    live["up2"] = by_rows(grad_hidden, full_fc1)
    step("fc1", "up2", "fc2")
    live["fc1"].core()
    grad_mid_norm, grad_gain2, grad_shift2 = norm_back(middle, gain2, shift2, live["up2"])
    grad_middle = grad_out + grad_mid_norm
    grad_branch = grad_middle.astype(bf16)
    grad_bias_out = jnp.sum(grad_branch.astype(f32), axis=0)
    live["grad_attended"] = by_rows(grad_branch, full_out).astype(bf16)
    live["out"] = Scatter(grid, attended, grad_branch)
    step("grad_attended", "out", "fc1", "fc2")
    live["fc2"].far_z()
    live["fc1"].first()
    live["out"].core()
    live["part"] = attend_back(
        info, starts, live["mixed"], live["other"], attended,
        jnp.concatenate([low_lse, high_lse]), live["grad_attended"], 0, 1,
    )
    step("part", "out", "fc1", "fc2", "active")
    dq, dkv, dkv_other = live["part"]
    live["fc2"].near_z()
    live["out"].first()
    live["back"] = grid.over_core(dkv_other)
    result = middle + jnp.dot(live["active"], full_fc2, preferred_element_type=f32) + b_fc2
    live["output"] = result.astype(bf16)
    step("back", "output", "out", "fc2", "fc1")
    live["fc1"].second()
    dk, dv = both(dkv, live["back"])
    grad_mixed = jnp.concatenate([dq, dk, dv], axis=1)
    live["grad_mixed"] = grad_mixed
    live["qkv"] = Scatter(grid, normed, grad_mixed)
    step("qkv", "grad_mixed", "fc1", "out", "output")
    live["qkv"].core()
    live["out"].second()
    output = swap_back(live["output"])
    live["up1"] = by_rows(live["grad_mixed"], full_qkv)
    step("qkv", "up1", "grad_mixed", "out")
    live["qkv"].first()
    live["fc1"].far_z()
    live["out"].far_z()
    grad_mixed = live["grad_mixed"]
    grad_bias_query = jnp.sum(grad_mixed[:, :width].astype(f32), axis=0)
    grad_bias_value = jnp.sum(grad_mixed[:, 2 * width :].astype(f32), axis=0)
    grad_in_norm, grad_gain1, grad_shift1 = norm_back(inputs, gain1, shift1, live["up1"])
    live["grad_tokens"] = (grad_middle + grad_in_norm).astype(bf16)
    sums = SumVectors(
        grid,
        jnp.concatenate(
            [
                v.reshape(-1, width)
                for v in (
                    grad_gain1, grad_shift1, grad_bias_query, grad_bias_value, grad_bias_out,
                    grad_gain2, grad_shift2, grad_bias_fc2, grad_bias_fc1,
                )
            ],
            axis=0,
        ),
    )
    live["sums"] = sums
    step("sums", "grad_tokens")
    sums.add(grid.over_core)
    sums.add(grid.over_x)
    step("sums", "qkv", "grad_tokens", "fc1", "out")
    live["qkv"].second()
    live["fc1"].near_z()
    live["out"].near_z()
    sums.add(grid.over_y)
    sums.add(lambda v: grid.flip_z(v, 1))
    step("sums", "qkv", "grad_tokens", "fc1", "out")
    live["qkv"].along_z()
    grad_tokens = swap_back(live["grad_tokens"])
    sums.add(lambda v: grid.flip_z(v, 2))
    sums = sums.state
    grad_qkv, grad_w_out, grad_fc1, grad_fc2 = (
        live[n].result() for n in ("qkv", "out", "fc1", "fc2")
    )

    device, devices = grid.f * n_tok + t, n_fsdp * n_tok

    def owned(vector):
        count = vector.shape[0] // devices
        return lax.dynamic_slice_in_dim(vector, device * count, count, 0)

    return (
        output,
        grad_tokens,
        owned(sums[0]),
        owned(sums[1]),
        grad_qkv,
        owned(sums[2]),
        owned(sums[3]),
        grad_w_out,
        owned(sums[4]),
        owned(sums[5]),
        owned(sums[6]),
        grad_fc1,
        owned(sums[8:].reshape(hidden_width)),
        grad_fc2,
        owned(sums[7]),
    )


def solution(mesh):
    vector, matrix = P("fsdp"), P("fsdp", None)
    rows = P(None, "fsdp", "tok", None)
    own_vector, own_matrix = P(("fsdp", "tok")), P(("fsdp", "tok"), None)
    return jax.shard_map(
        functools.partial(local, mesh.shape["fsdp"], mesh.shape["tok"]),
        mesh=mesh,
        in_specs=(
            rows, rows, P(None, "fsdp", None), vector, vector, matrix, vector, vector,
            matrix, vector, vector, vector, matrix, vector, matrix, vector,
        ),
        out_specs=(
            rows, rows, own_vector, own_vector, own_matrix, own_vector, own_vector,
            own_matrix, own_vector, own_vector, own_vector, own_matrix, own_vector,
            own_matrix, own_vector,
        ),
        check_vma=False,
    )
```

```python
import functools

import jax
import jax.numpy as jnp
from jax import lax
from jax.experimental import pallas as pl
from jax.experimental.pallas import tpu as pltpu
from jax.sharding import PartitionSpec as P

DH = 64
PAIR = 2 * DH
eps = 1e-05
masked_value = -1e30
f32 = jnp.float32
bf16 = jnp.bfloat16
AXES = ("fsdp", "tok")


class Grid:
    def __init__(self, n_fsdp, n_tok):
        self.n_fsdp, self.n_tok = n_fsdp, n_tok
        self.nz, self.ny = n_fsdp // 2, n_tok // 2
        self.f, self.t = lax.axis_index("fsdp"), lax.axis_index("tok")
        self.z, self.x = self.f // 2, self.f % 2
        self.y, self.c = self.t // 2, self.t % 2

    def staged(self, rows):
        return self.nz == 4 and self.ny == 2 and rows % 16 == 0

    def send(self, value, place):
        pairs = []
        for f in range(self.n_fsdp):
            for t in range(self.n_tok):
                z, x, y, c = place(f // 2, f % 2, t // 2, t % 2)
                pairs.append((f * self.n_tok + t, (z * 2 + x) * self.n_tok + y * 2 + c))
        return lax.ppermute(value, AXES, pairs)

    def over_core(self, value):
        return self.send(value, lambda z, x, y, c: (z, x, y, 1 - c))

    def over_x(self, value):
        return self.send(value, lambda z, x, y, c: (z, 1 - x, y, c))

    def over_y(self, value):
        return self.send(value, lambda z, x, y, c: (z, x, 1 - y, c))

    def over_yc(self, value):
        return self.send(value, lambda z, x, y, c: (z, x, 1 - y, 1 - c))

    def flip_z(self, value, bit):
        return self.send(value, lambda z, x, y, c: (z ^ bit, x, y, c))

    def over_z(self, value, shift):
        return self.send(value, lambda z, x, y, c: ((z + shift) % self.nz, x, y, c))


def pick(values, index, axis):
    return lax.dynamic_index_in_dim(values, index, axis, keepdims=False)


def both(a, b):
    return (a.astype(f32) + b.astype(f32)).astype(bf16)


def halves(a, b, index, lead=()):
    def part(values, i):
        rest = values.shape[len(lead) + 1 :]
        start = lead + (i,) + (0,) * len(rest)
        return lax.dynamic_slice(values, start, (1,) * (len(lead) + 1) + rest).reshape(rest)

    return both(part(a, index), part(b, index)), both(part(a, 1 - index), part(b, 1 - index))


def place_kernel(rows, widths, offsets, *refs):
    sem, outs, pieces = refs[-1], refs[-1 - len(widths) : -1], refs[: -1 - len(widths)]
    copies = []
    at = 0
    for piece in pieces:
        for j in range(piece.shape[0]):
            first = pl.multiple_of(offsets[at], rows)
            column = 0
            for i, width in enumerate(widths):
                copies.append(
                    pltpu.make_async_copy(
                        piece.at[j, :, pl.ds(column, width)],
                        outs[i].at[pl.ds(first, rows)],
                        sem.at[at * len(widths) + i],
                    )
                )
                column += width
            at += 1
    for copy in copies:
        copy.start()
    for copy in copies:
        copy.wait()


class Gather:
    def __init__(self, grid, *shards):
        self.grid, self.shards = grid, shards
        self.rows = shards[0].shape[0] // grid.n_tok
        self.staged = grid.staged(self.rows)
        self.state = {"shards": list(shards)}
        self.flip = True

    def own(self):
        parts = [
            lax.dynamic_slice_in_dim(w, self.grid.t * self.rows, self.rows, 0)
            for w in self.state["shards"]
        ]
        return jnp.concatenate(parts, axis=1)

    def along_z(self):
        if self.staged:
            own = self.own()
            self.flip = False
            self.state = {"steps": [own] + [self.grid.over_z(own, k) for k in (1, 2, 3)]}

    def beside_z(self):
        if self.staged:
            own = self.own()
            self.flip = False
            self.state = {"own": own, "z1": self.grid.over_z(own, 1), "z3": self.grid.over_z(own, 3)}

    def across_z(self):
        if self.staged:
            state = self.state
            self.state = {
                "steps": [state["own"], state["z1"], self.grid.over_z(state["own"], 2), state["z3"]]
            }

    def near_z(self):
        if self.staged:
            own = self.own()
            self.state = {"steps": [own, self.grid.flip_z(own, 1)]}

    def far_z(self):
        if self.staged:
            two = jnp.stack(self.state["steps"])
            self.state = {"steps": [two, self.grid.flip_z(two, 2)]}

    def first(self):
        if self.staged:
            grid, steps = self.grid, self.state["steps"]
            q = jnp.concatenate(steps) if self.flip else jnp.stack(steps)
            self.state = {"q": q, "x": [grid.over_x(q[:2])], "y": [grid.over_y(q[2:])]}

    def first_whole(self):
        if self.staged:
            grid, q = self.grid, jnp.stack(self.state["steps"])
            self.state = {"q": q, "x": [grid.over_x(q)], "y": [grid.over_y(q)]}

    def first_rest(self):
        if self.staged:
            grid, state = self.grid, self.state
            state["x"] = state["x"] + [grid.over_x(state["q"][2:])]
            state["y"] = [grid.over_y(state["q"][:2])] + state["y"]

    def second(self):
        if self.staged:
            state, grid = self.state, self.grid
            state["a"] = grid.over_y(state["x"][0][:2])
            state["b"] = grid.over_x(state["y"][-1][-2:])
            state["near"] = grid.over_core(
                jnp.concatenate([state["q"]] + state["x"] + state["y"])
            )

    def last(self):
        if self.staged:
            state = self.state
            state["cab"] = self.grid.over_core(jnp.concatenate([state["a"], state["b"]]))

    def place(self):
        if not self.staged:
            return [lax.all_gather(w, "fsdp", axis=0, tiled=True) for w in self.state["shards"]]
        grid, rows = self.grid, self.rows
        shard_rows, kind = self.shards[0].shape[0], self.shards[0].dtype
        widths = [w.shape[1] for w in self.shards]
        at = lambda dx, dy: [(k, dx, dy) for k in range(4)]
        ab = at(1, 1)
        order = (
            ("q", at(0, 0), 0), ("x", at(1, 0), 0), ("y", at(0, 1), 0), ("a", ab[:2], 0),
            ("b", ab[2:], 0), ("near", at(0, 0) + at(1, 0) + at(0, 1), 1), ("cab", ab, 1),
        )
        offsets, pieces = [], []
        for name, places, dc in order:
            have = self.state[name]
            pieces += have if isinstance(have, (list, tuple)) else [have]
            for k, dx, dy in places:
                z = grid.z ^ k if self.flip else (grid.z + 4 - k) % 4
                x, y, c = grid.x ^ dx, grid.y ^ dy, grid.c ^ dc
                offsets.append((z * 2 + x) * shard_rows + (y * 2 + c) * rows)
        total = grid.n_fsdp * shard_rows
        return pl.pallas_call(
            functools.partial(place_kernel, rows, widths),
            out_shape=[jax.ShapeDtypeStruct((total, width), kind) for width in widths],
            in_specs=[pl.BlockSpec(memory_space=pltpu.SMEM)]
            + [pl.BlockSpec(memory_space=pl.ANY)] * len(pieces),
            out_specs=[pl.BlockSpec(memory_space=pltpu.VMEM)] * len(widths),
            scratch_shapes=[pltpu.SemaphoreType.DMA((len(offsets) * len(widths),))],
            compiler_params=pltpu.CompilerParams(vmem_limit_bytes=24 * 2**20),
            cost_estimate=pl.CostEstimate(
                flops=0, bytes_accessed=4 * total * sum(widths), transcendentals=0
            ),
            name="place",
        )(jnp.stack(offsets).astype(jnp.int32), *pieces)


class GatherVectors:
    def __init__(self, grid, packed):
        self.grid, self.staged = grid, grid.nz == 4
        self.state = packed

    def over_x(self):
        if not self.staged:
            self.state = lax.all_gather(self.state, "fsdp", axis=0)
            return
        whole = jnp.zeros((self.grid.n_fsdp,) + self.state.shape, self.state.dtype)
        whole = lax.dynamic_update_index_in_dim(whole, self.state, self.grid.f, 0)
        self.state = whole + self.grid.over_x(whole)

    def over_z(self, bit):
        if self.staged:
            self.state = self.state + self.grid.flip_z(self.state, bit)


def split_kernel(rows, core, left, right, own, other, turned):
    @pl.when(pl.program_id(1) == 0)
    def turn():
        turned[...] = left[...].T

    tile = own.shape[-1]
    columns = pl.ds(pl.multiple_of(pl.program_id(1) * tile, tile), tile)
    total = jnp.dot(turned[...], right[:, columns], preferred_element_type=f32).astype(bf16)
    first = core[0] == 0

    def put(order):
        for x in range(2):
            for y in range(2):
                at = (x * 2 + y) * 2 * rows
                low, high = total[at : at + rows], total[at + rows : at + 2 * rows]
                i, j = (x, y) if order else (y, x)
                own[0, i, j, 0] = jnp.where(first, low, high)
                other[0, i, j, 0] = jnp.where(first, high, low)

    z = pl.program_id(0)
    pl.when(z < 2)(lambda: put(True))
    pl.when(z >= 2)(lambda: put(False))


class Scatter:
    def __init__(self, grid, left, right):
        self.grid = grid
        count, height, width = left.shape + right.shape[1:]
        rows = height // (grid.n_fsdp * grid.n_tok)
        self.staged = grid.staged(rows)
        if not self.staged:
            self.state = by_columns(left, right)
            return
        tile = min(width, 1024 if rows <= 32 else 512)
        part = jax.ShapeDtypeStruct((2, 2, 2, 2, rows, width), bf16)
        block = pl.BlockSpec(
            (1, 2, 2, 1, rows, tile), lambda z, n, core: (z // 2, 0, 0, z % 2, 0, n)
        )
        self.state = pl.pallas_call(
            functools.partial(split_kernel, rows),
            out_shape=(part, part),
            grid_spec=pltpu.PrefetchScalarGridSpec(
                num_scalar_prefetch=1,
                grid=(4, width // tile),
                in_specs=[
                    pl.BlockSpec((count, 8 * rows), lambda z, n, core: (0, z)),
                    pl.BlockSpec((count, width), lambda z, n, core: (0, 0)),
                ],
                out_specs=[block, block],
                scratch_shapes=[pltpu.VMEM((8 * rows, count), bf16)],
            ),
            compiler_params=pltpu.CompilerParams(vmem_limit_bytes=32 * 2**20),
            cost_estimate=pl.CostEstimate(
                flops=2 * count * height * width,
                bytes_accessed=2 * (height * width + count * (height + width)),
                transcendentals=0,
            ),
            name="grad_split",
        )(grid.c[None].astype(jnp.int32), left, right)

    def core(self):
        if self.staged:
            own, other = self.state
            self.state = (own, self.grid.over_core(other))

    def first(self):
        if self.staged:
            grid, (own, more) = self.grid, self.state
            ka, sa = halves(own, more, grid.x, (0,))
            kb, sb = halves(own, more, grid.y, (1,))
            self.state = (ka, grid.over_x(sa), kb, grid.over_y(sb))

    def second(self):
        if self.staged:
            grid, (ka, ma, kb, mb) = self.grid, self.state
            ka, sa = halves(ka, ma, grid.y)
            kb, sb = halves(kb, mb, grid.x)
            self.state = (ka, grid.over_y(sa), kb, grid.over_x(sb))

    def far_z(self):
        if self.staged:
            low, (ka, ma, kb, mb) = self.grid.z < 2, self.state
            a, b = both(ka, ma), both(kb, mb)
            self.state = (jnp.where(low, a, b), self.grid.flip_z(jnp.where(low, b, a), 2))

    def near_z(self):
        if self.staged:
            keep, send = halves(*self.state, self.grid.z % 2)
            self.state = (keep, self.grid.flip_z(send, 1))

    def along_z(self):
        if self.staged:
            z, (ka, ma, kb, mb) = self.grid.z, self.state
            last = jnp.concatenate([both(ka, ma), both(kb, mb)])
            self.state = (pick(last, z, 0),) + tuple(
                self.grid.over_z(pick(last, (z + shift) % 4, 0), shift) for shift in (1, 2, 3)
            )

    def result(self):
        if not self.staged:
            return lax.psum_scatter(self.state, AXES, scatter_dimension=0, tiled=True)
        total = self.state[0].astype(f32)
        for more in self.state[1:]:
            total = total + more.astype(f32)
        return total


class SumVectors:
    def __init__(self, grid, packed):
        self.grid, self.staged = grid, grid.nz == 4 and grid.ny == 2
        self.state = packed if self.staged else lax.psum(packed, AXES)

    def add(self, over):
        if self.staged:
            self.state = self.state + over(self.state)


def layer_norm(values, gain, shift):
    mean = jnp.mean(values, axis=-1, keepdims=True)
    centered = values - mean
    spread = jnp.mean(centered * centered, axis=-1, keepdims=True)
    return centered * lax.rsqrt(spread + eps) * gain + shift


def norm_back(values, gain, shift, upstream):
    result, pull = jax.vjp(layer_norm, values, gain, shift)
    return pull(upstream)


def smooth_gate(values):
    return jax.nn.gelu(values, approximate=True)


def by_rows(a, b):
    return lax.dot_general(a, b, (((1,), (1,)), ((), ())), preferred_element_type=f32)


def by_columns(a, b):
    return lax.dot_general(a, b, (((0,), (0,)), ((), ())), preferred_element_type=f32)


def fill(info, own, other, whole, block):
    for j in range(2):
        rows = slice(j * block, (j + 1) * block)
        whole[pl.ds(pl.multiple_of(info[j] * block, block), block), :] = own[rows, :]
        whole[pl.ds(pl.multiple_of(info[2 + j] * block, block), block), :] = other[rows, :]


def head_part(values, h):
    lane = lax.broadcasted_iota(jnp.int32, values.shape, 1)
    return jnp.where(lane // DH == h, values, jnp.zeros_like(values))


def keep_mask(starts, index, first, keys, block):
    key_pos = lax.broadcasted_iota(jnp.int32, (keys, block), 0)
    query_pos = first + lax.broadcasted_iota(jnp.int32, (1, block), 1)
    start = starts[pl.ds(index, 1), :]
    return (key_pos >= start) & (key_pos <= query_pos)


def attend_kernel(block, info, starts, q, k, v, ko, vo, out, lse, kn, vn):
    fill(info, k, ko, kn, block)
    fill(info, v, vo, vn, block)

    def run(index, count):
        at = pl.ds(pl.multiple_of(index * block, block), block)
        keys, vals = kn[: count * block, :], vn[: count * block, :]
        query = q[at, :] * jnp.asarray(DH**-0.5, bf16)
        keep = keep_mask(starts, index, info[index] * block, count * block, block)
        sides = []
        for h in range(2):
            scores = jnp.where(keep, by_rows(keys, head_part(query, h)), masked_value)
            top = jnp.max(scores, axis=0, keepdims=True)
            expo = jnp.exp(scores - top)
            total = jnp.sum(expo, axis=0, keepdims=True)
            lse[0, pl.ds(2 * h + index, 1), :] = top + jnp.log(total)
            side = by_columns(vals, expo.astype(bf16)) / total
            sides.append(side[h * DH : (h + 1) * DH])
        out[at, :] = jnp.concatenate(sides, axis=0).T.astype(bf16)

    low = info[4]
    for index, counts in ((low, (1, 2)), (1 - low, (3, 4))):
        for count in counts:
            pl.when(info[index] == count - 1)(functools.partial(run, index, count))


def attend_back_kernel(
    block, info, starts, q, k, v, ko, vo, out, lse, grad, dq, dkv, dkvo, kn, vn, dkn, dvn
):
    fill(info, k, ko, kn, block)
    fill(info, v, vo, vn, block)
    dkn[...] = jnp.zeros_like(dkn)
    dvn[...] = jnp.zeros_like(dvn)

    def run(index, count):
        at = pl.ds(pl.multiple_of(index * block, block), block)
        keys, vals = kn[: count * block, :], vn[: count * block, :]
        query = q[at, :] * jnp.asarray(DH**-0.5, bf16)
        up = grad[at, :]
        product = (up.astype(f32) * out[at, :].astype(f32)).T
        keep = keep_mask(starts, index, info[index] * block, count * block, block)
        sides = []
        for h in range(2):
            query_h, up_h = head_part(query, h), head_part(up, h)
            inner = jnp.sum(product[h * DH : (h + 1) * DH], axis=0, keepdims=True)
            scores = jnp.where(keep, by_rows(keys, query_h), masked_value)
            probs = jnp.exp(scores - lse[0, pl.ds(2 * h + index, 1), :])
            grad_scores = (probs * (by_rows(vals, up_h) - inner)).astype(bf16)
            dvn[: count * block, :] += jnp.dot(
                probs.astype(bf16), up_h, preferred_element_type=f32
            )
            dkn[: count * block, :] += jnp.dot(grad_scores, query_h, preferred_element_type=f32)
            side = by_columns(keys, grad_scores) * DH**-0.5
            sides.append(side[h * DH : (h + 1) * DH])
        dq[at, :] = jnp.concatenate(sides, axis=0).T.astype(bf16)

    low = info[4]
    for index, counts in ((low, (1, 2)), (1 - low, (3, 4))):
        for count in counts:
            pl.when(info[index] == count - 1)(functools.partial(run, index, count))
    for j in range(2):
        rows = slice(j * block, (j + 1) * block)
        own = pl.ds(pl.multiple_of(info[j] * block, block), block)
        other = pl.ds(pl.multiple_of(info[2 + j] * block, block), block)
        for i, whole in enumerate((dkn, dvn)):
            dkv[i, rows, :] = whole[own, :]
            dkvo[i, rows, :] = whole[other, :].astype(bf16)


def attend_specs(count, width, at):
    pairs = width // PAIR
    return [
        pl.BlockSpec((2, count // 2), lambda h, info: (0, 0)),
        pl.BlockSpec((count, PAIR), lambda h, info: (0, at + h)),
        pl.BlockSpec((count, PAIR), lambda h, info: (0, pairs + at + h)),
        pl.BlockSpec((count, PAIR), lambda h, info: (0, 2 * pairs + at + h)),
        pl.BlockSpec((count, PAIR), lambda h, info: (0, at + h)),
        pl.BlockSpec((count, PAIR), lambda h, info: (0, pairs + at + h)),
    ]


def attend(info, starts, mixed, other, part, parts):
    count, width = mixed.shape[0], mixed.shape[1] // 3
    pairs, block = width // PAIR // parts, count // 2
    column = pl.BlockSpec((count, PAIR), lambda h, info: (0, h))
    return pl.pallas_call(
        functools.partial(attend_kernel, block),
        out_shape=(
            jax.ShapeDtypeStruct((count, width // parts), bf16),
            jax.ShapeDtypeStruct((pairs, 4, block), f32),
        ),
        grid_spec=pltpu.PrefetchScalarGridSpec(
            num_scalar_prefetch=1,
            grid=(pairs,),
            in_specs=attend_specs(count, width, part * pairs),
            out_specs=[column, pl.BlockSpec((1, 4, block), lambda h, info: (h, 0, 0))],
            scratch_shapes=[pltpu.VMEM((2 * count, PAIR), bf16)] * 2,
        ),
        compiler_params=pltpu.CompilerParams(vmem_limit_bytes=32 * 2**20),
        cost_estimate=pl.CostEstimate(
            flops=8 * count * count * width // parts, bytes_accessed=12 * count * width // parts,
            transcendentals=20 * count * count // parts,
        ),
        name="attend",
    )(info, starts, mixed, mixed, mixed, other, other)


def attend_back(info, starts, mixed, other, attended, lse, grad, part, parts):
    count, width = grad.shape
    pairs, block = width // PAIR // parts, count // 2
    column = pl.BlockSpec((count, PAIR), lambda h, info: (0, h))
    return pl.pallas_call(
        functools.partial(attend_back_kernel, block),
        out_shape=(
            jax.ShapeDtypeStruct((count, width // parts), bf16),
            jax.ShapeDtypeStruct((2, count, width // parts), f32),
            jax.ShapeDtypeStruct((2, count, width // parts), bf16),
        ),
        grid_spec=pltpu.PrefetchScalarGridSpec(
            num_scalar_prefetch=1,
            grid=(pairs,),
            in_specs=attend_specs(count, width, part * pairs)
            + [
                column,
                pl.BlockSpec((1, 4, block), lambda h, info: (h, 0, 0)),
                pl.BlockSpec((count, PAIR), lambda h, info: (0, part * pairs + h)),
            ],
            out_specs=[column] + [pl.BlockSpec((2, count, PAIR), lambda h, info: (0, 0, h))] * 2,
            scratch_shapes=[pltpu.VMEM((2 * count, PAIR), bf16)] * 2
            + [pltpu.VMEM((2 * count, PAIR), f32)] * 2,
        ),
        compiler_params=pltpu.CompilerParams(vmem_limit_bytes=32 * 2**20),
        cost_estimate=pl.CostEstimate(
            flops=20 * count * count * width // parts, bytes_accessed=28 * count * width // parts,
            transcendentals=20 * count * count // parts,
        ),
        name="attend_back",
    )(info, starts, mixed, mixed, mixed, other, other, attended, lse, grad)


def local(
    n_fsdp,
    n_tok,
    tokens,
    cotangent,
    doc_lengths,
    norm1_gain,
    norm1_shift,
    w_qkv,
    bias_query,
    bias_value,
    w_out,
    bias_out,
    norm2_gain,
    norm2_shift,
    w_fc1,
    bias_fc1,
    w_fc2,
    bias_fc2,
):
    grid = Grid(n_fsdp, n_tok)
    y, t = grid.y, grid.t
    block, width = tokens.shape[2:]
    hidden_width = w_fc1.shape[1]

    def swap(values):
        mine, theirs = pick(values, y, 0)[0], pick(values, 1 - y, 0)[0]
        return jnp.concatenate([mine, grid.over_yc(theirs)], axis=0)

    def swap_back(values, back=None):
        mine = values[:block]
        back = grid.over_yc(values[block:]) if back is None else back
        first, second = jnp.where(y == 0, mine, back), jnp.where(y == 0, back, mine)
        return jnp.stack([first, second])[:, None]

    live = {}
    kinds = (Gather, Scatter, GatherVectors, SumVectors)

    def step(*names):
        moving = [live[n].state if isinstance(live[n], kinds) else live[n] for n in names]
        for name, value in zip(names, lax.optimization_barrier(moving)):
            if isinstance(live[name], kinds):
                live[name].state = value
            else:
                live[name] = value

    vectors = (
        norm1_gain, norm1_shift, bias_query, bias_value, bias_out, norm2_gain, norm2_shift, bias_fc2
    )
    part = norm1_gain.shape[0]
    packed = jnp.concatenate([v[None] for v in vectors] + [bias_fc1.reshape(-1, part)], axis=0)
    w1, w2, w3, small = (
        Gather(grid, w_qkv), Gather(grid, w_out, w_fc1), Gather(grid, w_fc2), GatherVectors(grid, packed)
    )
    live.update(w1=w1, w2=w2, w3=w3, small=small)

    mine, across = jnp.stack([t, 3 - t]), jnp.stack([t ^ 1, 3 - (t ^ 1)])
    info = jnp.concatenate([mine, across, y[None]]).astype(jnp.int32)
    lengths = pick(doc_lengths, y, 0)[0]
    ends = jnp.cumsum(lengths)
    place = mine[:, None] * block + jnp.arange(block, dtype=jnp.int32)[None]
    starts = jnp.max(
        jnp.where(place[..., None] >= ends, ends, 0), axis=-1
    ).astype(jnp.int32)

    w1.along_z()
    live["rows"], live["up"] = swap(tokens), swap(cotangent)
    step("w1", "rows", "up", "small", "w2")
    w1.first_whole()
    w2.beside_z()
    small.over_x()
    step("w1", "w2", "small")
    w1.second()
    w2.across_z()
    small.over_z(1)
    step("w1", "w2", "small", "w3")
    w1.last()
    w2.first()
    small.over_z(2)
    packed = small.state
    gain1, shift1, b_query, b_value, b_out, gain2, shift2, b_fc2 = (
        packed[:, i].reshape(width).astype(f32) for i in range(8)
    )
    b_fc1 = packed[:, 8:].reshape(hidden_width).astype(f32)
    inputs = live["rows"].astype(f32)
    live["normed"] = layer_norm(inputs, gain1, shift1).astype(bf16)
    step("w1", "normed", "w3")
    w3.beside_z()
    (full_qkv,) = w1.place()
    b_qkv = jnp.concatenate([b_query, jnp.zeros_like(b_query), b_value])
    normed = live["normed"]
    live["mixed"] = (jnp.dot(normed, full_qkv, preferred_element_type=f32) + b_qkv).astype(bf16)
    step("mixed", "w3", "w2")
    w2.first_rest()
    live["other"] = grid.over_core(live["mixed"][:, width:])
    step("mixed", "other")
    w3.across_z()
    low, low_lse = attend(info, starts, live["mixed"], live["other"], 0, 2)
    live["low"] = low
    step("low", "other", "mixed", "w2", "w3")
    w2.second()
    high, high_lse = attend(info, starts, live["mixed"], live["other"], 1, 2)
    live["high"] = high
    step("high", "w2", "w3")
    w2.last()
    w3.first()
    attended = jnp.concatenate([live["low"], live["high"]], axis=1)
    live["attended"] = attended
    step("w2", "attended")
    attended = live["attended"]
    full_out, full_fc1 = w2.place()
    middle = inputs + jnp.dot(attended, full_out, preferred_element_type=f32) + b_out
    live["middle"] = middle
    live["normed2"] = layer_norm(middle, gain2, shift2).astype(bf16)
    live["hidden"] = jnp.dot(live["normed2"], full_fc1, preferred_element_type=f32) + b_fc1
    step("hidden", "normed2", "middle", "w3")
    w3.first_rest()
    normed2, middle, upstream = live["normed2"], live["middle"], live["up"]
    live["active"] = smooth_gate(live["hidden"]).astype(bf16)
    live["fc2"] = Scatter(grid, live["active"], upstream)
    step("fc2", "active", "hidden", "w3")
    w3.second()
    live["fc2"].core()
    step("fc2", "hidden", "w3")

    w3.last()
    step("w3", "hidden")
    live["fc2"].first()
    (full_fc2,) = w3.place()
    grad_out = upstream.astype(f32)
    grad_bias_fc2 = jnp.sum(grad_out, axis=0)
    unused, gate_pull = jax.vjp(smooth_gate, live["hidden"])
    grad_hidden = gate_pull(by_rows(upstream, full_fc2))[0].astype(bf16)
    live["grad_hidden"] = grad_hidden
    grad_bias_fc1 = jnp.sum(grad_hidden.astype(f32), axis=0)
    step("grad_hidden", "fc2")
    live["fc2"].second()
    grad_hidden = live["grad_hidden"]
    live["fc1"] = Scatter(grid, normed2, grad_hidden)
    live["up2"] = by_rows(grad_hidden, full_fc1)
    step("fc1", "up2", "fc2")
    live["fc1"].core()
    grad_mid_norm, grad_gain2, grad_shift2 = norm_back(middle, gain2, shift2, live["up2"])
    grad_middle = grad_out + grad_mid_norm
    grad_branch = grad_middle.astype(bf16)
    grad_bias_out = jnp.sum(grad_branch.astype(f32), axis=0)
    live["grad_attended"] = by_rows(grad_branch, full_out).astype(bf16)
    live["out"] = Scatter(grid, attended, grad_branch)
    step("grad_attended", "out", "fc1", "fc2")
    live["fc2"].far_z()
    live["fc1"].first()
    live["out"].core()
    live["part"] = attend_back(
        info, starts, live["mixed"], live["other"], attended,
        jnp.concatenate([low_lse, high_lse]), live["grad_attended"], 0, 1,
    )
    step("part", "out", "fc1", "fc2", "active")
    dq, dkv, dkv_other = live["part"]
    live["fc2"].near_z()
    live["out"].first()
    live["back"] = grid.over_core(dkv_other)
    result = middle + jnp.dot(live["active"], full_fc2, preferred_element_type=f32) + b_fc2
    live["output"] = result.astype(bf16)
    step("back", "output", "out", "fc2", "fc1")
    live["fc1"].second()
    dk, dv = both(dkv, live["back"])
    grad_mixed = jnp.concatenate([dq, dk, dv], axis=1)
    live["grad_mixed"] = grad_mixed
    live["qkv"] = Scatter(grid, normed, grad_mixed)
    step("qkv", "grad_mixed", "fc1", "out", "output")
    live["qkv"].core()
    live["out"].second()
    live["back"] = grid.over_yc(live["output"][block:])
    live["up1"] = by_rows(live["grad_mixed"], full_qkv)
    step("qkv", "up1", "grad_mixed", "out", "back")
    output = swap_back(live["output"], live["back"])
    live["qkv"].first()
    live["fc1"].far_z()
    live["out"].far_z()
    grad_mixed = live["grad_mixed"]
    grad_bias_query = jnp.sum(grad_mixed[:, :width].astype(f32), axis=0)
    grad_bias_value = jnp.sum(grad_mixed[:, 2 * width :].astype(f32), axis=0)
    grad_in_norm, grad_gain1, grad_shift1 = norm_back(inputs, gain1, shift1, live["up1"])
    live["grad_tokens"] = (grad_middle + grad_in_norm).astype(bf16)
    sums = SumVectors(
        grid,
        jnp.concatenate(
            [
                v.reshape(-1, width)
                for v in (
                    grad_gain1, grad_shift1, grad_bias_query, grad_bias_value, grad_bias_out,
                    grad_gain2, grad_shift2, grad_bias_fc2, grad_bias_fc1,
                )
            ],
            axis=0,
        ),
    )
    live["sums"] = sums
    step("sums", "grad_tokens")
    sums.add(grid.over_core)
    sums.add(grid.over_x)
    step("sums", "qkv", "grad_tokens", "fc1", "out")
    live["qkv"].second()
    live["fc1"].near_z()
    live["out"].near_z()
    sums.add(grid.over_y)
    sums.add(lambda v: grid.flip_z(v, 1))
    sums.add(lambda v: grid.flip_z(v, 2))
    step("sums", "qkv", "grad_tokens", "fc1", "out")
    live["qkv"].along_z()
    grad_tokens = swap_back(live["grad_tokens"])
    sums = sums.state
    grad_qkv, grad_w_out, grad_fc1, grad_fc2 = (
        live[n].result() for n in ("qkv", "out", "fc1", "fc2")
    )

    device, devices = grid.f * n_tok + t, n_fsdp * n_tok

    def owned(vector):
        count = vector.shape[0] // devices
        return lax.dynamic_slice_in_dim(vector, device * count, count, 0)

    return (
        output,
        grad_tokens,
        owned(sums[0]),
        owned(sums[1]),
        grad_qkv,
        owned(sums[2]),
        owned(sums[3]),
        grad_w_out,
        owned(sums[4]),
        owned(sums[5]),
        owned(sums[6]),
        grad_fc1,
        owned(sums[8:].reshape(hidden_width)),
        grad_fc2,
        owned(sums[7]),
    )


def solution(mesh):
    vector, matrix = P("fsdp"), P("fsdp", None)
    rows = P(None, "fsdp", "tok", None)
    own_vector, own_matrix = P(("fsdp", "tok")), P(("fsdp", "tok"), None)
    return jax.shard_map(
        functools.partial(local, mesh.shape["fsdp"], mesh.shape["tok"]),
        mesh=mesh,
        in_specs=(
            rows, rows, P(None, "fsdp", None), vector, vector, matrix, vector, vector,
            matrix, vector, vector, vector, matrix, vector, matrix, vector,
        ),
        out_specs=(
            rows, rows, own_vector, own_vector, own_matrix, own_vector, own_vector,
            own_matrix, own_vector, own_vector, own_vector, own_matrix, own_vector,
            own_matrix, own_vector,
        ),
        check_vma=False,
    )
```

```python
import functools

import jax
import jax.numpy as jnp
from jax import lax
from jax.experimental import pallas as pl
from jax.experimental.pallas import tpu as pltpu
from jax.sharding import PartitionSpec as P

DH = 64
PAIR = 2 * DH
eps = 1e-05
masked_value = -1e30
f32 = jnp.float32
bf16 = jnp.bfloat16
AXES = ("fsdp", "tok")


class Grid:
    def __init__(self, n_fsdp, n_tok):
        self.n_fsdp, self.n_tok = n_fsdp, n_tok
        self.nz, self.ny = n_fsdp // 2, n_tok // 2
        self.f, self.t = lax.axis_index("fsdp"), lax.axis_index("tok")
        self.z, self.x = self.f // 2, self.f % 2
        self.y, self.c = self.t // 2, self.t % 2

    def staged(self, rows):
        return self.nz == 4 and self.ny == 2 and rows % 16 == 0

    def send(self, value, place):
        pairs = []
        for f in range(self.n_fsdp):
            for t in range(self.n_tok):
                z, x, y, c = place(f // 2, f % 2, t // 2, t % 2)
                pairs.append((f * self.n_tok + t, (z * 2 + x) * self.n_tok + y * 2 + c))
        return lax.ppermute(value, AXES, pairs)

    def over_core(self, value):
        return self.send(value, lambda z, x, y, c: (z, x, y, 1 - c))

    def over_x(self, value):
        return self.send(value, lambda z, x, y, c: (z, 1 - x, y, c))

    def over_y(self, value):
        return self.send(value, lambda z, x, y, c: (z, x, 1 - y, c))

    def over_yc(self, value):
        return self.send(value, lambda z, x, y, c: (z, x, 1 - y, 1 - c))

    def flip_z(self, value, bit):
        return self.send(value, lambda z, x, y, c: (z ^ bit, x, y, c))

    def over_z(self, value, shift):
        return self.send(value, lambda z, x, y, c: ((z + shift) % self.nz, x, y, c))


def pick(values, index, axis):
    return lax.dynamic_index_in_dim(values, index, axis, keepdims=False)


def both(a, b):
    return (a.astype(f32) + b.astype(f32)).astype(bf16)


def halves(a, b, index, lead=()):
    def part(values, i):
        rest = values.shape[len(lead) + 1 :]
        start = lead + (i,) + (0,) * len(rest)
        return lax.dynamic_slice(values, start, (1,) * (len(lead) + 1) + rest).reshape(rest)

    return both(part(a, index), part(b, index)), both(part(a, 1 - index), part(b, 1 - index))


def place_kernel(rows, widths, offsets, *refs):
    sem, outs, pieces = refs[-1], refs[-1 - len(widths) : -1], refs[: -1 - len(widths)]
    copies = []
    at = 0
    for piece in pieces:
        for j in range(piece.shape[0]):
            first = pl.multiple_of(offsets[at], rows)
            column = 0
            for i, width in enumerate(widths):
                copies.append(
                    pltpu.make_async_copy(
                        piece.at[j, :, pl.ds(column, width)],
                        outs[i].at[pl.ds(first, rows)],
                        sem.at[at * len(widths) + i],
                    )
                )
                column += width
            at += 1
    for copy in copies:
        copy.start()
    for copy in copies:
        copy.wait()


class Gather:
    def __init__(self, grid, *shards):
        self.grid, self.shards = grid, shards
        self.rows = shards[0].shape[0] // grid.n_tok
        self.staged = grid.staged(self.rows)
        self.state = {"shards": list(shards)}
        self.flip = True

    def own(self):
        parts = [
            lax.dynamic_slice_in_dim(w, self.grid.t * self.rows, self.rows, 0)
            for w in self.state["shards"]
        ]
        return jnp.concatenate(parts, axis=1)

    def along_z(self):
        if self.staged:
            own = self.own()
            self.flip = False
            self.state = {"steps": [own] + [self.grid.over_z(own, k) for k in (1, 2, 3)]}

    def beside_z(self):
        if self.staged:
            own = self.own()
            self.flip = False
            self.state = {"own": own, "z1": self.grid.over_z(own, 1), "z3": self.grid.over_z(own, 3)}

    def across_z(self):
        if self.staged:
            state = self.state
            self.state = {
                "steps": [state["own"], state["z1"], self.grid.over_z(state["own"], 2), state["z3"]]
            }

    def near_z(self):
        if self.staged:
            own = self.own()
            self.state = {"steps": [own, self.grid.flip_z(own, 1)]}

    def far_z(self):
        if self.staged:
            two = jnp.stack(self.state["steps"])
            self.state = {"steps": [two, self.grid.flip_z(two, 2)]}

    def first(self):
        if self.staged:
            grid, steps = self.grid, self.state["steps"]
            q = jnp.concatenate(steps) if self.flip else jnp.stack(steps)
            self.state = {"q": q, "x": [grid.over_x(q[:2])], "y": [grid.over_y(q[2:])]}

    def first_whole(self):
        if self.staged:
            grid, q = self.grid, jnp.stack(self.state["steps"])
            self.state = {"q": q, "x": [grid.over_x(q)], "y": [grid.over_y(q)]}

    def first_rest(self):
        if self.staged:
            grid, state = self.grid, self.state
            state["x"] = state["x"] + [grid.over_x(state["q"][2:])]
            state["y"] = [grid.over_y(state["q"][:2])] + state["y"]

    def second(self):
        if self.staged:
            state, grid = self.state, self.grid
            state["a"] = grid.over_y(state["x"][0][:2])
            state["b"] = grid.over_x(state["y"][-1][-2:])
            state["near"] = grid.over_core(
                jnp.concatenate([state["q"]] + state["x"] + state["y"])
            )

    def last(self):
        if self.staged:
            state = self.state
            state["cab"] = self.grid.over_core(jnp.concatenate([state["a"], state["b"]]))

    def place(self):
        if not self.staged:
            return [lax.all_gather(w, "fsdp", axis=0, tiled=True) for w in self.state["shards"]]
        grid, rows = self.grid, self.rows
        shard_rows, kind = self.shards[0].shape[0], self.shards[0].dtype
        widths = [w.shape[1] for w in self.shards]
        at = lambda dx, dy: [(k, dx, dy) for k in range(4)]
        ab = at(1, 1)
        order = (
            ("q", at(0, 0), 0), ("x", at(1, 0), 0), ("y", at(0, 1), 0), ("a", ab[:2], 0),
            ("b", ab[2:], 0), ("near", at(0, 0) + at(1, 0) + at(0, 1), 1), ("cab", ab, 1),
        )
        offsets, pieces = [], []
        for name, places, dc in order:
            have = self.state[name]
            pieces += have if isinstance(have, (list, tuple)) else [have]
            for k, dx, dy in places:
                z = grid.z ^ k if self.flip else (grid.z + 4 - k) % 4
                x, y, c = grid.x ^ dx, grid.y ^ dy, grid.c ^ dc
                offsets.append((z * 2 + x) * shard_rows + (y * 2 + c) * rows)
        total = grid.n_fsdp * shard_rows
        return pl.pallas_call(
            functools.partial(place_kernel, rows, widths),
            out_shape=[jax.ShapeDtypeStruct((total, width), kind) for width in widths],
            in_specs=[pl.BlockSpec(memory_space=pltpu.SMEM)]
            + [pl.BlockSpec(memory_space=pl.ANY)] * len(pieces),
            out_specs=[pl.BlockSpec(memory_space=pltpu.VMEM)] * len(widths),
            scratch_shapes=[pltpu.SemaphoreType.DMA((len(offsets) * len(widths),))],
            compiler_params=pltpu.CompilerParams(vmem_limit_bytes=24 * 2**20),
            cost_estimate=pl.CostEstimate(
                flops=0, bytes_accessed=4 * total * sum(widths), transcendentals=0
            ),
            name="place",
        )(jnp.stack(offsets).astype(jnp.int32), *pieces)


class GatherVectors:
    def __init__(self, grid, packed):
        self.grid, self.staged = grid, grid.nz == 4
        self.state = packed

    def over_x(self):
        if not self.staged:
            self.state = lax.all_gather(self.state, "fsdp", axis=0)
            return
        whole = jnp.zeros((self.grid.n_fsdp,) + self.state.shape, self.state.dtype)
        whole = lax.dynamic_update_index_in_dim(whole, self.state, self.grid.f, 0)
        self.state = whole + self.grid.over_x(whole)

    def over_z(self, bit):
        if self.staged:
            self.state = self.state + self.grid.flip_z(self.state, bit)


def split_kernel(rows, core, left, right, own, other, turned):
    @pl.when(pl.program_id(1) == 0)
    def turn():
        turned[...] = left[...].T

    tile = own.shape[-1]
    columns = pl.ds(pl.multiple_of(pl.program_id(1) * tile, tile), tile)
    total = jnp.dot(turned[...], right[:, columns], preferred_element_type=f32).astype(bf16)
    first = core[0] == 0

    def put(order):
        for x in range(2):
            for y in range(2):
                at = (x * 2 + y) * 2 * rows
                low, high = total[at : at + rows], total[at + rows : at + 2 * rows]
                i, j = (x, y) if order else (y, x)
                own[0, i, j, 0] = jnp.where(first, low, high)
                other[0, i, j, 0] = jnp.where(first, high, low)

    z = pl.program_id(0)
    pl.when(z < 2)(lambda: put(True))
    pl.when(z >= 2)(lambda: put(False))


class Scatter:
    def __init__(self, grid, left, right):
        self.grid = grid
        count, height, width = left.shape + right.shape[1:]
        rows = height // (grid.n_fsdp * grid.n_tok)
        self.staged = grid.staged(rows)
        if not self.staged:
            self.state = by_columns(left, right)
            return
        tile = min(width, 1024 if rows <= 32 else 512)
        part = jax.ShapeDtypeStruct((2, 2, 2, 2, rows, width), bf16)
        block = pl.BlockSpec(
            (1, 2, 2, 1, rows, tile), lambda z, n, core: (z // 2, 0, 0, z % 2, 0, n)
        )
        self.state = pl.pallas_call(
            functools.partial(split_kernel, rows),
            out_shape=(part, part),
            grid_spec=pltpu.PrefetchScalarGridSpec(
                num_scalar_prefetch=1,
                grid=(4, width // tile),
                in_specs=[
                    pl.BlockSpec((count, 8 * rows), lambda z, n, core: (0, z)),
                    pl.BlockSpec((count, width), lambda z, n, core: (0, 0)),
                ],
                out_specs=[block, block],
                scratch_shapes=[pltpu.VMEM((8 * rows, count), bf16)],
            ),
            compiler_params=pltpu.CompilerParams(vmem_limit_bytes=32 * 2**20),
            cost_estimate=pl.CostEstimate(
                flops=2 * count * height * width,
                bytes_accessed=2 * (height * width + count * (height + width)),
                transcendentals=0,
            ),
            name="grad_split",
        )(grid.c[None].astype(jnp.int32), left, right)

    def core(self):
        if self.staged:
            own, other = self.state
            self.state = (own, self.grid.over_core(other))

    def first(self):
        if self.staged:
            grid, (own, more) = self.grid, self.state
            ka, sa = halves(own, more, grid.x, (0,))
            kb, sb = halves(own, more, grid.y, (1,))
            self.state = (ka, grid.over_x(sa), kb, grid.over_y(sb))

    def second(self):
        if self.staged:
            grid, (ka, ma, kb, mb) = self.grid, self.state
            ka, sa = halves(ka, ma, grid.y)
            kb, sb = halves(kb, mb, grid.x)
            self.state = (ka, grid.over_y(sa), kb, grid.over_x(sb))

    def far_z(self):
        if self.staged:
            low, (ka, ma, kb, mb) = self.grid.z < 2, self.state
            a, b = both(ka, ma), both(kb, mb)
            self.state = (jnp.where(low, a, b), self.grid.flip_z(jnp.where(low, b, a), 2))

    def near_z(self):
        if self.staged:
            keep, send = halves(*self.state, self.grid.z % 2)
            self.state = (keep, self.grid.flip_z(send, 1))

    def along_z(self):
        if self.staged:
            z, (ka, ma, kb, mb) = self.grid.z, self.state
            last = jnp.concatenate([both(ka, ma), both(kb, mb)])
            self.state = (pick(last, z, 0),) + tuple(
                self.grid.over_z(pick(last, (z + shift) % 4, 0), shift) for shift in (1, 2, 3)
            )

    def result(self):
        if not self.staged:
            return lax.psum_scatter(self.state, AXES, scatter_dimension=0, tiled=True)
        total = self.state[0].astype(f32)
        for more in self.state[1:]:
            total = total + more.astype(f32)
        return total


class SumVectors:
    def __init__(self, grid, packed):
        self.grid, self.staged = grid, grid.nz == 4 and grid.ny == 2
        self.state = packed if self.staged else lax.psum(packed, AXES)

    def add(self, over):
        if self.staged:
            self.state = self.state + over(self.state)


def layer_norm(values, gain, shift):
    mean = jnp.mean(values, axis=-1, keepdims=True)
    centered = values - mean
    spread = jnp.mean(centered * centered, axis=-1, keepdims=True)
    return centered * lax.rsqrt(spread + eps) * gain + shift


def norm_back(values, gain, shift, upstream):
    result, pull = jax.vjp(layer_norm, values, gain, shift)
    return pull(upstream)


def smooth_gate(values):
    return jax.nn.gelu(values, approximate=True)


def by_rows(a, b):
    return lax.dot_general(a, b, (((1,), (1,)), ((), ())), preferred_element_type=f32)


def by_columns(a, b):
    return lax.dot_general(a, b, (((0,), (0,)), ((), ())), preferred_element_type=f32)


def fill(info, own, other, whole, block):
    for j in range(2):
        rows = slice(j * block, (j + 1) * block)
        whole[pl.ds(pl.multiple_of(info[j] * block, block), block), :] = own[rows, :]
        whole[pl.ds(pl.multiple_of(info[2 + j] * block, block), block), :] = other[rows, :]


def head_part(values, h):
    lane = lax.broadcasted_iota(jnp.int32, values.shape, 1)
    return jnp.where(lane // DH == h, values, jnp.zeros_like(values))


def keep_mask(starts, index, first, keys, block):
    key_pos = lax.broadcasted_iota(jnp.int32, (keys, block), 0)
    query_pos = first + lax.broadcasted_iota(jnp.int32, (1, block), 1)
    start = starts[pl.ds(index, 1), :]
    return (key_pos >= start) & (key_pos <= query_pos)


def attend_kernel(block, info, starts, q, k, v, ko, vo, out, lse, kn, vn):
    fill(info, k, ko, kn, block)
    fill(info, v, vo, vn, block)

    def run(index, count):
        at = pl.ds(pl.multiple_of(index * block, block), block)
        keys, vals = kn[: count * block, :], vn[: count * block, :]
        query = q[at, :] * jnp.asarray(DH**-0.5, bf16)
        keep = keep_mask(starts, index, info[index] * block, count * block, block)
        sides = []
        for h in range(2):
            scores = jnp.where(keep, by_rows(keys, head_part(query, h)), masked_value)
            top = jnp.max(scores, axis=0, keepdims=True)
            expo = jnp.exp(scores - top)
            total = jnp.sum(expo, axis=0, keepdims=True)
            lse[0, pl.ds(2 * h + index, 1), :] = top + jnp.log(total)
            side = by_columns(vals, expo.astype(bf16)) / total
            sides.append(side[h * DH : (h + 1) * DH])
        out[at, :] = jnp.concatenate(sides, axis=0).T.astype(bf16)

    low = info[4]
    for index, counts in ((low, (1, 2)), (1 - low, (3, 4))):
        for count in counts:
            pl.when(info[index] == count - 1)(functools.partial(run, index, count))


def attend_back_kernel(
    block, info, starts, q, k, v, ko, vo, out, lse, grad, dq, dkv, dkvo, kn, vn, dkn, dvn
):
    fill(info, k, ko, kn, block)
    fill(info, v, vo, vn, block)
    dkn[...] = jnp.zeros_like(dkn)
    dvn[...] = jnp.zeros_like(dvn)

    def run(index, count):
        at = pl.ds(pl.multiple_of(index * block, block), block)
        keys, vals = kn[: count * block, :], vn[: count * block, :]
        query = q[at, :] * jnp.asarray(DH**-0.5, bf16)
        up = grad[at, :]
        product = (up.astype(f32) * out[at, :].astype(f32)).T
        keep = keep_mask(starts, index, info[index] * block, count * block, block)
        sides = []
        for h in range(2):
            query_h, up_h = head_part(query, h), head_part(up, h)
            inner = jnp.sum(product[h * DH : (h + 1) * DH], axis=0, keepdims=True)
            scores = jnp.where(keep, by_rows(keys, query_h), masked_value)
            probs = jnp.exp(scores - lse[0, pl.ds(2 * h + index, 1), :])
            grad_scores = (probs * (by_rows(vals, up_h) - inner)).astype(bf16)
            dvn[: count * block, :] += jnp.dot(
                probs.astype(bf16), up_h, preferred_element_type=f32
            )
            dkn[: count * block, :] += jnp.dot(grad_scores, query_h, preferred_element_type=f32)
            side = by_columns(keys, grad_scores) * DH**-0.5
            sides.append(side[h * DH : (h + 1) * DH])
        dq[at, :] = jnp.concatenate(sides, axis=0).T.astype(bf16)

    low = info[4]
    for index, counts in ((low, (1, 2)), (1 - low, (3, 4))):
        for count in counts:
            pl.when(info[index] == count - 1)(functools.partial(run, index, count))
    for j in range(2):
        rows = slice(j * block, (j + 1) * block)
        own = pl.ds(pl.multiple_of(info[j] * block, block), block)
        other = pl.ds(pl.multiple_of(info[2 + j] * block, block), block)
        for i, whole in enumerate((dkn, dvn)):
            dkv[i, rows, :] = whole[own, :]
            dkvo[i, rows, :] = whole[other, :].astype(bf16)


def attend_specs(count, width, at):
    pairs = width // PAIR
    return [
        pl.BlockSpec((2, count // 2), lambda h, info: (0, 0)),
        pl.BlockSpec((count, PAIR), lambda h, info: (0, at + h)),
        pl.BlockSpec((count, PAIR), lambda h, info: (0, pairs + at + h)),
        pl.BlockSpec((count, PAIR), lambda h, info: (0, 2 * pairs + at + h)),
        pl.BlockSpec((count, PAIR), lambda h, info: (0, at + h)),
        pl.BlockSpec((count, PAIR), lambda h, info: (0, pairs + at + h)),
    ]


def attend(info, starts, mixed, other, part, parts):
    count, width = mixed.shape[0], mixed.shape[1] // 3
    pairs, block = width // PAIR // parts, count // 2
    column = pl.BlockSpec((count, PAIR), lambda h, info: (0, h))
    return pl.pallas_call(
        functools.partial(attend_kernel, block),
        out_shape=(
            jax.ShapeDtypeStruct((count, width // parts), bf16),
            jax.ShapeDtypeStruct((pairs, 4, block), f32),
        ),
        grid_spec=pltpu.PrefetchScalarGridSpec(
            num_scalar_prefetch=1,
            grid=(pairs,),
            in_specs=attend_specs(count, width, part * pairs),
            out_specs=[column, pl.BlockSpec((1, 4, block), lambda h, info: (h, 0, 0))],
            scratch_shapes=[pltpu.VMEM((2 * count, PAIR), bf16)] * 2,
        ),
        compiler_params=pltpu.CompilerParams(vmem_limit_bytes=32 * 2**20),
        cost_estimate=pl.CostEstimate(
            flops=8 * count * count * width // parts, bytes_accessed=12 * count * width // parts,
            transcendentals=20 * count * count // parts,
        ),
        name="attend",
    )(info, starts, mixed, mixed, mixed, other, other)


def attend_back(info, starts, mixed, other, attended, lse, grad, part, parts):
    count, width = grad.shape
    pairs, block = width // PAIR // parts, count // 2
    column = pl.BlockSpec((count, PAIR), lambda h, info: (0, h))
    return pl.pallas_call(
        functools.partial(attend_back_kernel, block),
        out_shape=(
            jax.ShapeDtypeStruct((count, width // parts), bf16),
            jax.ShapeDtypeStruct((2, count, width // parts), f32),
            jax.ShapeDtypeStruct((2, count, width // parts), bf16),
        ),
        grid_spec=pltpu.PrefetchScalarGridSpec(
            num_scalar_prefetch=1,
            grid=(pairs,),
            in_specs=attend_specs(count, width, part * pairs)
            + [
                column,
                pl.BlockSpec((1, 4, block), lambda h, info: (h, 0, 0)),
                pl.BlockSpec((count, PAIR), lambda h, info: (0, part * pairs + h)),
            ],
            out_specs=[column] + [pl.BlockSpec((2, count, PAIR), lambda h, info: (0, 0, h))] * 2,
            scratch_shapes=[pltpu.VMEM((2 * count, PAIR), bf16)] * 2
            + [pltpu.VMEM((2 * count, PAIR), f32)] * 2,
        ),
        compiler_params=pltpu.CompilerParams(vmem_limit_bytes=32 * 2**20),
        cost_estimate=pl.CostEstimate(
            flops=20 * count * count * width // parts, bytes_accessed=28 * count * width // parts,
            transcendentals=20 * count * count // parts,
        ),
        name="attend_back",
    )(info, starts, mixed, mixed, mixed, other, other, attended, lse, grad)


def local(
    n_fsdp,
    n_tok,
    tokens,
    cotangent,
    doc_lengths,
    norm1_gain,
    norm1_shift,
    w_qkv,
    bias_query,
    bias_value,
    w_out,
    bias_out,
    norm2_gain,
    norm2_shift,
    w_fc1,
    bias_fc1,
    w_fc2,
    bias_fc2,
):
    grid = Grid(n_fsdp, n_tok)
    y, t = grid.y, grid.t
    block, width = tokens.shape[2:]
    hidden_width = w_fc1.shape[1]

    def swap(values):
        mine, theirs = pick(values, y, 0)[0], pick(values, 1 - y, 0)[0]
        return jnp.concatenate([mine, grid.over_yc(theirs)], axis=0)

    def swap_back(values, back=None):
        mine = values[:block]
        back = grid.over_yc(values[block:]) if back is None else back
        first, second = jnp.where(y == 0, mine, back), jnp.where(y == 0, back, mine)
        return jnp.stack([first, second])[:, None]

    live = {}
    kinds = (Gather, Scatter, GatherVectors, SumVectors)

    def step(*names):
        moving = [live[n].state if isinstance(live[n], kinds) else live[n] for n in names]
        for name, value in zip(names, lax.optimization_barrier(moving)):
            if isinstance(live[name], kinds):
                live[name].state = value
            else:
                live[name] = value

    vectors = (
        norm1_gain, norm1_shift, bias_query, bias_value, bias_out, norm2_gain, norm2_shift, bias_fc2
    )
    part = norm1_gain.shape[0]
    packed = jnp.concatenate([v[None] for v in vectors] + [bias_fc1.reshape(-1, part)], axis=0)
    w1, w2, w3, small = (
        Gather(grid, w_qkv), Gather(grid, w_out, w_fc1), Gather(grid, w_fc2), GatherVectors(grid, packed)
    )
    live.update(w1=w1, w2=w2, w3=w3, small=small)

    mine, across = jnp.stack([t, 3 - t]), jnp.stack([t ^ 1, 3 - (t ^ 1)])
    info = jnp.concatenate([mine, across, y[None]]).astype(jnp.int32)
    lengths = pick(doc_lengths, y, 0)[0]
    ends = jnp.cumsum(lengths)
    place = mine[:, None] * block + jnp.arange(block, dtype=jnp.int32)[None]
    starts = jnp.max(
        jnp.where(place[..., None] >= ends, ends, 0), axis=-1
    ).astype(jnp.int32)

    w1.along_z()
    live["rows"] = swap(tokens)
    small.over_x()
    live["later"] = cotangent
    step("w1", "rows", "small", "w2", "later")
    w1.first_whole()
    w2.beside_z()
    small.over_z(1)
    step("w1", "w2", "small", "later")
    w1.second()
    w2.across_z()
    live["up"] = swap(live["later"])
    step("w1", "w2", "small", "w3", "up")
    w1.last()
    w2.first()
    small.over_z(2)
    packed = small.state
    gain1, shift1, b_query, b_value, b_out, gain2, shift2, b_fc2 = (
        packed[:, i].reshape(width).astype(f32) for i in range(8)
    )
    b_fc1 = packed[:, 8:].reshape(hidden_width).astype(f32)
    inputs = live["rows"].astype(f32)
    live["normed"] = layer_norm(inputs, gain1, shift1).astype(bf16)
    step("w1", "normed", "w3")
    w3.beside_z()
    (full_qkv,) = w1.place()
    b_qkv = jnp.concatenate([b_query, jnp.zeros_like(b_query), b_value])
    normed = live["normed"]
    live["mixed"] = (jnp.dot(normed, full_qkv, preferred_element_type=f32) + b_qkv).astype(bf16)
    step("mixed", "w3", "w2")
    w2.first_rest()
    live["other"] = grid.over_core(live["mixed"][:, width:])
    step("mixed", "other")
    w3.across_z()
    low, low_lse = attend(info, starts, live["mixed"], live["other"], 0, 2)
    live["low"] = low
    step("low", "other", "mixed", "w2", "w3")
    w2.second()
    high, high_lse = attend(info, starts, live["mixed"], live["other"], 1, 2)
    live["high"] = high
    step("high", "w2", "w3")
    w2.last()
    w3.first()
    attended = jnp.concatenate([live["low"], live["high"]], axis=1)
    live["attended"] = attended
    step("w2", "attended")
    attended = live["attended"]
    full_out, full_fc1 = w2.place()
    middle = inputs + jnp.dot(attended, full_out, preferred_element_type=f32) + b_out
    live["middle"] = middle
    live["normed2"] = layer_norm(middle, gain2, shift2).astype(bf16)
    live["hidden"] = jnp.dot(live["normed2"], full_fc1, preferred_element_type=f32) + b_fc1
    step("hidden", "normed2", "middle", "w3")
    w3.first_rest()
    normed2, middle, upstream = live["normed2"], live["middle"], live["up"]
    live["active"] = smooth_gate(live["hidden"]).astype(bf16)
    live["fc2"] = Scatter(grid, live["active"], upstream)
    step("fc2", "active", "hidden", "w3")
    w3.second()
    live["fc2"].core()
    step("fc2", "hidden", "w3")

    w3.last()
    step("w3", "hidden")
    live["fc2"].first()
    (full_fc2,) = w3.place()
    grad_out = upstream.astype(f32)
    grad_bias_fc2 = jnp.sum(grad_out, axis=0)
    unused, gate_pull = jax.vjp(smooth_gate, live["hidden"])
    grad_hidden = gate_pull(by_rows(upstream, full_fc2))[0].astype(bf16)
    live["grad_hidden"] = grad_hidden
    grad_bias_fc1 = jnp.sum(grad_hidden.astype(f32), axis=0)
    step("grad_hidden", "fc2")
    live["fc2"].second()
    grad_hidden = live["grad_hidden"]
    live["fc1"] = Scatter(grid, normed2, grad_hidden)
    live["up2"] = by_rows(grad_hidden, full_fc1)
    step("fc1", "up2", "fc2")
    live["fc1"].core()
    grad_mid_norm, grad_gain2, grad_shift2 = norm_back(middle, gain2, shift2, live["up2"])
    grad_middle = grad_out + grad_mid_norm
    grad_branch = grad_middle.astype(bf16)
    grad_bias_out = jnp.sum(grad_branch.astype(f32), axis=0)
    live["grad_attended"] = by_rows(grad_branch, full_out).astype(bf16)
    live["out"] = Scatter(grid, attended, grad_branch)
    step("grad_attended", "out", "fc1", "fc2")
    live["fc2"].far_z()
    live["fc1"].first()
    live["out"].core()
    live["part"] = attend_back(
        info, starts, live["mixed"], live["other"], attended,
        jnp.concatenate([low_lse, high_lse]), live["grad_attended"], 0, 1,
    )
    step("part", "out", "fc1", "fc2", "active")
    dq, dkv, dkv_other = live["part"]
    live["fc2"].near_z()
    live["out"].first()
    live["back"] = grid.over_core(dkv_other)
    result = middle + jnp.dot(live["active"], full_fc2, preferred_element_type=f32) + b_fc2
    live["output"] = result.astype(bf16)
    step("back", "output", "out", "fc2", "fc1")
    live["fc1"].second()
    dk, dv = both(dkv, live["back"])
    grad_mixed = jnp.concatenate([dq, dk, dv], axis=1)
    live["grad_mixed"] = grad_mixed
    live["qkv"] = Scatter(grid, normed, grad_mixed)
    step("qkv", "grad_mixed", "fc1", "out", "output")
    live["qkv"].core()
    live["out"].second()
    live["back"] = grid.over_yc(live["output"][block:])
    live["up1"] = by_rows(live["grad_mixed"], full_qkv)
    step("qkv", "up1", "grad_mixed", "out", "back")
    output = swap_back(live["output"], live["back"])
    live["qkv"].first()
    live["fc1"].far_z()
    live["out"].far_z()
    grad_mixed = live["grad_mixed"]
    grad_bias_query = jnp.sum(grad_mixed[:, :width].astype(f32), axis=0)
    grad_bias_value = jnp.sum(grad_mixed[:, 2 * width :].astype(f32), axis=0)
    grad_in_norm, grad_gain1, grad_shift1 = norm_back(inputs, gain1, shift1, live["up1"])
    live["grad_tokens"] = (grad_middle + grad_in_norm).astype(bf16)
    sums = SumVectors(
        grid,
        jnp.concatenate(
            [
                v.reshape(-1, width)
                for v in (
                    grad_gain1, grad_shift1, grad_bias_query, grad_bias_value, grad_bias_out,
                    grad_gain2, grad_shift2, grad_bias_fc2, grad_bias_fc1,
                )
            ],
            axis=0,
        ),
    )
    live["sums"] = sums
    step("sums", "grad_tokens")
    sums.add(grid.over_core)
    sums.add(grid.over_x)
    step("sums", "qkv", "grad_tokens", "fc1", "out")
    live["qkv"].second()
    live["fc1"].near_z()
    live["out"].near_z()
    sums.add(grid.over_y)
    sums.add(lambda v: grid.flip_z(v, 1))
    sums.add(lambda v: grid.flip_z(v, 2))
    step("sums", "qkv", "grad_tokens", "fc1", "out")
    live["qkv"].along_z()
    grad_tokens = swap_back(live["grad_tokens"])
    sums = sums.state
    grad_qkv, grad_w_out, grad_fc1, grad_fc2 = (
        live[n].result() for n in ("qkv", "out", "fc1", "fc2")
    )

    device, devices = grid.f * n_tok + t, n_fsdp * n_tok

    def owned(vector):
        count = vector.shape[0] // devices
        return lax.dynamic_slice_in_dim(vector, device * count, count, 0)

    return (
        output,
        grad_tokens,
        owned(sums[0]),
        owned(sums[1]),
        grad_qkv,
        owned(sums[2]),
        owned(sums[3]),
        grad_w_out,
        owned(sums[4]),
        owned(sums[5]),
        owned(sums[6]),
        grad_fc1,
        owned(sums[8:].reshape(hidden_width)),
        grad_fc2,
        owned(sums[7]),
    )


def solution(mesh):
    vector, matrix = P("fsdp"), P("fsdp", None)
    rows = P(None, "fsdp", "tok", None)
    own_vector, own_matrix = P(("fsdp", "tok")), P(("fsdp", "tok"), None)
    return jax.shard_map(
        functools.partial(local, mesh.shape["fsdp"], mesh.shape["tok"]),
        mesh=mesh,
        in_specs=(
            rows, rows, P(None, "fsdp", None), vector, vector, matrix, vector, vector,
            matrix, vector, vector, vector, matrix, vector, matrix, vector,
        ),
        out_specs=(
            rows, rows, own_vector, own_vector, own_matrix, own_vector, own_vector,
            own_matrix, own_vector, own_vector, own_vector, own_matrix, own_vector,
            own_matrix, own_vector,
        ),
        check_vma=False,
    )
```
